32 devices in a mesh: dp: 4 (over z), space: 8 (over y, x, core).
Axes of the slice: x: 2, y: 2, z: 4, core: 2. Of those that a mesh axis runs over, the one named last changes fastest.
Arguments:
- universes: bfloat16 [4, 16, 16, 16, 128], P('dp', 'space'), may hold values from -6 to 6
- conv_weight: bfloat16 [3456, 128], replicated, may hold values from -0.109375 to 0.109375
- mix_weight: bfloat16 [128, 256], replicated, may hold values from -0.5 to 0.5
- feature_grad: bfloat16 [4, 16, 16, 16, 256], P('dp', 'space'), may hold values from -6 to 6
Outputs:
- features: bfloat16 [4, 16, 16, 16, 256], P('dp', 'space')
- input_grad: bfloat16 [4, 16, 16, 16, 128], P('dp', 'space')
- weight_grads: float32 [475136], P(('dp', 'space'))
The draws below stay inside these ranges and needn't reach their ends.
All inputs are finite; a program needn't handle non-finite values.
Results may differ from the reference program's by a relative error of at most 0.015.
Values may be sent and summed in bfloat16 or wider, within the bound.
No kernel may reach another device: no remote copies, remote signals or barrier semaphores. Data moves between devices by JAX's collectives and lax.ppermute only.
A program may use at most 64 MiB of HBM per device.

```python
import jax
import jax.numpy as jnp
from jax import lax

C = 128
F = 256
NY = 16
NZ = 16
TAPS = 27
NX = 16
BATCH = 4
NORMALIZER = 32
GRADS = 475136


def shard_levels(key, shape, cuts, low, largest):
    def one(position, blocks):
        draws = jax.random.uniform(jax.random.fold_in(jax.random.fold_in(key, 6), position), (blocks,), jnp.float32, low / len(cuts), largest / len(cuts))
        return jnp.repeat(jnp.exp(draws), shape[position] // blocks).reshape((-1,) + (1,) * (len(shape) - position - 1))

    gain = one(*cuts[0])
    for cut in cuts[1:]:
        gain = gain * one(*cut)
    return gain


def gaussian(rng, shape, deviation, most, cuts=(), dtype=jnp.bfloat16):
    result = deviation * jax.random.normal(rng, shape, jnp.float32)
    if cuts:
        result = result * shard_levels(rng, shape, cuts, -0.22, 0.18)
    return jnp.clip(result, -most, most).astype(dtype)


def setup_inputs(seed: int = 0) -> dict:
    seeds = jax.random.split(jax.random.key(seed), 5)
    return {
        "universes": gaussian(seeds[0], (BATCH, NX, NY, NZ, C), 1.0, 6.0, ((0, 4), (1, 8))),
        "conv_weight": gaussian(seeds[1], (TAPS * C, C), (TAPS * C) ** -0.5, 0.109375),
        "mix_weight": gaussian(seeds[2], (C, F), C ** -0.5, 0.5),
        "feature_grad": gaussian(seeds[3], (BATCH, NX, NY, NZ, F), 1.0, 6.0, ((0, 4), (1, 8))),
    }


leak_slope = 0.3


def cell_patches(volume, mirror):
    padded = jnp.pad(volume, ((1, 1), (1, 1), (1, 1), (0, 0)))
    planes, row_count, columns = volume.shape[0], volume.shape[1], volume.shape[2]
    pieces = []
    for first in range(3):
        for second in range(3):
            for third in range(3):
                if mirror:
                    start_a, start_b, start_c = 2 - first, 2 - second, 2 - third
                else:
                    start_a, start_b, start_c = first, second, third
                pieces.append(padded[start_a:start_a + planes, start_b:start_b + row_count, start_c:start_c + columns, :])
    joined = jnp.concatenate(pieces, axis=-1)
    return joined.reshape(planes * row_count * columns, joined.shape[-1])


def reference(universes, conv_weight, mix_weight, feature_grad):
    kernel = conv_weight.astype(jnp.float32)
    flipped = jnp.transpose(kernel.reshape(TAPS, C, C), (0, 2, 1)).reshape(TAPS * C, C)
    mixing = mix_weight.astype(jnp.float32)
    highest = lax.Precision.HIGHEST

    def one_universe(totals, pair):
        sample, incoming = pair
        volume = sample.astype(jnp.float32)
        forward_patch = cell_patches(volume, False)
        summed = jnp.dot(forward_patch, kernel, precision=highest)
        hidden = lax.optimization_barrier(jnp.where(summed > 0, summed, leak_slope * summed).astype(jnp.bfloat16)).astype(jnp.float32)
        features = jnp.dot(hidden, mixing, precision=highest).astype(jnp.bfloat16)
        upstream = incoming.astype(jnp.float32).reshape(-1, F)
        pulled = jnp.dot(upstream, mixing.T, precision=highest)
        hidden_grad = lax.optimization_barrier((pulled * jnp.where(summed > 0, 1.0, leak_slope)).astype(jnp.bfloat16)).astype(jnp.float32)
        grad_patch = cell_patches(hidden_grad.reshape(NX, NY, NZ, C), True)
        volume_grad = jnp.dot(grad_patch, flipped, precision=highest)
        kernel_grad = jnp.dot(forward_patch.T, hidden_grad, precision=highest)
        mix_grad = jnp.dot(hidden.T, upstream, precision=highest)
        new_totals = (totals[0] + kernel_grad, totals[1] + mix_grad)
        return new_totals, (features.reshape(NX, NY, NZ, F), volume_grad.astype(jnp.bfloat16).reshape(NX, NY, NZ, C))

    initial = (jnp.zeros((TAPS * C, C), jnp.float32), jnp.zeros((C, F), jnp.float32))
    totals, outputs = lax.scan(one_universe, initial, (universes, feature_grad))
    padding = jnp.zeros((GRADS - TAPS * C * C - C * F,), jnp.float32)
    flattened = jnp.concatenate([totals[0].reshape(-1), totals[1].reshape(-1), padding]) / NORMALIZER
    return outputs[0], outputs[1], flattened
```

```python
import functools

import jax
import jax.numpy as jnp
from jax import lax
from jax.experimental import pallas as pl
from jax.experimental.pallas import tpu as pltpu
from jax.sharding import PartitionSpec as P

leak_slope = 0.3
bf16 = jnp.bfloat16
f32 = jnp.float32
NT = (((1,), (1,)), ((), ()))
TN = (((0,), (0,)), ((), ()))
VMEM = pl.BlockSpec(memory_space=pltpu.VMEM)
HBM = pl.BlockSpec(memory_space=pl.ANY)


def shift_columns(value, step, columns):
    rows = value.shape[0]
    place = lax.rem(lax.broadcasted_iota(jnp.int32, value.shape, 0), columns)
    moved = pltpu.roll(value, step % rows, 0)
    edge = 0 if step == 1 else columns - 1
    return jnp.where(place == edge, 0.0, moved)


def gather_rows(target, row_start, column_start, source, row_shift, columns):
    cells, width = source.shape
    lanes = pl.ds(column_start, width)
    if row_shift == 0:
        target[pl.ds(row_start, cells), lanes] = source[...]
    elif row_shift < 0:
        target[pl.ds(row_start, columns), lanes] = jnp.zeros((columns, width), source.dtype)
        target[pl.ds(row_start + columns, cells - columns), lanes] = source[pl.ds(0, cells - columns), :]
    else:
        target[pl.ds(row_start, cells - columns), lanes] = source[pl.ds(columns, cells - columns), :]
        target[pl.ds(row_start + cells - columns, columns), lanes] = jnp.zeros((columns, width), source.dtype)


def forward_kernel(columns, order, x_ref, low_ref, high_ref, w_ref, mix_ref, fg_ref,
                   hidden_ref, hg_ref, grads_ref, patch, wide, cotangents, rows_ref, sems):
    planes, cells, channels = x_ref.shape
    width = mix_ref.shape[1]
    copies = []
    for e in range(3):
        copy = pltpu.make_async_copy(
            w_ref.at[:, e], wide.at[:, :, pl.ds(e * channels, channels)], sems.at[e]
        )
        copy.start()
        copies.append(copy)
    for p in range(planes):
        for a in range(3):
            source = p + a - 1
            ref = low_ref if source < 0 else high_ref if source >= planes else x_ref.at[source]
            for b in range(3):
                gather_rows(patch, p * cells, (a * 3 + b) * channels, ref, b - 1, columns)
    for copy in copies:
        copy.wait()
    weights = wide[...].reshape(9 * channels, 3 * channels)
    for p in range(planes):
        rows = pl.ds(p * cells, cells)
        parts = jnp.dot(patch[rows, :], weights, preferred_element_type=f32)
        summed = (
            parts[:, channels : 2 * channels]
            + shift_columns(parts[:, :channels], 1, columns)
            + shift_columns(parts[:, 2 * channels :], -1, columns)
        )
        hidden_ref[p] = jnp.where(summed > 0, summed, leak_slope * summed).astype(bf16)
        pulled = lax.dot_general(fg_ref[p], mix_ref[...], NT, preferred_element_type=f32)
        hg = (pulled * jnp.where(summed > 0, 1.0, leak_slope)).astype(bf16)
        hg_ref[p] = hg
        wide_hg = hg.astype(f32)
        cotangents[rows, pl.ds(0, channels)] = shift_columns(wide_hg, -1, columns).astype(bf16)
        cotangents[rows, pl.ds(channels, channels)] = hg
        cotangents[rows, pl.ds(2 * channels, channels)] = shift_columns(wide_hg, 1, columns).astype(bf16)
    taps = 27 * channels
    mixed = jnp.zeros((channels, width), f32)
    for p in range(planes):
        mixed = mixed + lax.dot_general(hidden_ref[p], fg_ref[p], TN, preferred_element_type=f32)
    parts_of_mix = width // channels
    for j in range(parts_of_mix):
        rows_ref[pl.ds(taps + j, channels, stride=parts_of_mix), :] = mixed[:, j * channels : (j + 1) * channels]
    for ab in range(9):
        block = lax.dot_general(
            patch[:, pl.ds(ab * channels, channels)], cotangents[...], TN, preferred_element_type=f32
        )
        for e in range(3):
            rows_ref[pl.ds((ab * 3 + e) * channels, channels), :] = block[:, e * channels : (e + 1) * channels]
    if order is None:
        grads_ref[...] = rows_ref[...].astype(bf16)
    else:
        piece = grads_ref.shape[1]
        for k in range(grads_ref.shape[0]):
            grads_ref[order(k)] = rows_ref[pl.ds(k * piece, piece), :].astype(bf16)


def backward_kernel(columns, hg_ref, low_ref, high_ref, w_ref, hidden_ref, mix_ref,
                    features_ref, input_ref, patch):
    planes, cells, channels = hg_ref.shape
    for p in range(planes):
        features_ref[p] = jnp.dot(hidden_ref[p], mix_ref[...], preferred_element_type=f32).astype(bf16)
        for a in range(3):
            source = p + 1 - a
            ref = low_ref if source < 0 else high_ref if source >= planes else hg_ref.at[source]
            for b in range(3):
                gather_rows(patch, p * cells, (a * 3 + b) * channels, ref, 1 - b, columns)
    for p in range(planes):
        parts = jnp.zeros((cells, 3 * channels), f32)
        for first in range(0, 9, 2):
            count = min(2, 9 - first)
            block = jnp.concatenate([w_ref[first + i] for i in range(count)], axis=1)
            parts = parts + lax.dot_general(
                patch[pl.ds(p * cells, cells), pl.ds(first * channels, count * channels)],
                block, NT, preferred_element_type=f32,
            )
        total = (
            parts[:, channels : 2 * channels]
            + shift_columns(parts[:, :channels], -1, columns)
            + shift_columns(parts[:, 2 * channels :], 1, columns)
        )
        input_ref[p] = total.astype(bf16)


def digits_of(count):
    digits = []
    while count > 1:
        for radix in (2, 3, 5, 7, count) if not digits else (4, 2, 3, 5, 7, count):
            if count % radix == 0:
                digits.append(radix)
                count //= radix
                break
    return digits


def stages_of(axis, digits):
    stages, stride = [], 1
    for radix in digits:
        stages.append((axis, stride, radix))
        stride *= radix
    return stages


def turned(count, stride, radix, k):
    pairs = []
    for i in range(count):
        digit = i // stride % radix
        pairs.append((i, i + ((digit + k) % radix - digit) * stride))
    return pairs


def halos(volume, axis):
    count = lax.axis_size(axis)
    forward = [(i, i + 1) for i in range(count - 1)]
    backward = [(i + 1, i) for i in range(count - 1)]
    low = lax.ppermute(volume[-1], axis, forward)
    high = lax.ppermute(volume[0], axis, backward)
    return low, high


def shards(universes, conv_weight, mix_weight, feature_grad):
    channels = conv_weight.shape[1]
    width = mix_weight.shape[1]
    planes, map_rows, columns = universes.shape[1:4]
    cells = map_rows * columns
    group_count, slab_count = lax.axis_size("dp"), lax.axis_size("space")
    devices = group_count * slab_count
    space_digits = digits_of(slab_count)
    dp_digits = [4] if group_count == 4 else digits_of(group_count)
    stages = stages_of("space", space_digits) + stages_of("dp", dp_digits)

    x = universes.reshape(planes, cells, channels)
    fg = feature_grad.reshape(planes, cells, width)
    weights = conv_weight.reshape(9, 3, channels, channels)
    low, high = halos(x, "space")

    total_rows = 27 * channels + channels * width // channels
    share = (total_rows * channels + devices - 1) // devices
    aligned = share * devices == total_rows * channels and share % channels == 0
    if aligned:
        piece = share // channels
        grads_shape = (devices, piece, channels)

        def order(k):
            place = 0
            for axis, stride, radix in stages:
                index = k % slab_count if axis == "space" else k // slab_count
                mine = lax.rem(lax.axis_index(axis) // stride, radix)
                place = place * radix + lax.rem(index // stride % radix - mine + radix, radix)
            return place
    else:
        grads_shape = (total_rows, channels)
        order = None

    flops = 2 * planes * cells * channels * (2 * 27 * channels + 2 * width)
    hidden, hg, grads = pl.pallas_call(
        functools.partial(forward_kernel, columns, order),
        out_shape=(
            jax.ShapeDtypeStruct((planes, cells, channels), bf16),
            jax.ShapeDtypeStruct((planes, cells, channels), bf16),
            jax.ShapeDtypeStruct(grads_shape, bf16),
        ),
        in_specs=[VMEM, VMEM, VMEM, HBM, VMEM, VMEM],
        out_specs=(VMEM, VMEM, VMEM),
        scratch_shapes=[
            pltpu.VMEM((planes * cells, 9 * channels), bf16),
            pltpu.VMEM((9, channels, 3 * channels), bf16),
            pltpu.VMEM((planes * cells, 3 * channels), bf16),
            pltpu.VMEM((total_rows, channels), f32),
            pltpu.SemaphoreType.DMA((3,)),
        ],
        compiler_params=pltpu.CompilerParams(vmem_limit_bytes=24 * 1024 * 1024),
        cost_estimate=pl.CostEstimate(flops=flops, bytes_accessed=3_000_000, transcendentals=0),
        name="forward_and_kernel_grads",
    )(x, low, high, weights, mix_weight, fg)

    hg_low, hg_high = halos(hg, "space")
    features, input_grad = pl.pallas_call(
        functools.partial(backward_kernel, columns),
        out_shape=(
            jax.ShapeDtypeStruct((planes, cells, width), bf16),
            jax.ShapeDtypeStruct((planes, cells, channels), bf16),
        ),
        in_specs=[VMEM] * 6,
        out_specs=(VMEM, VMEM),
        scratch_shapes=[pltpu.VMEM((planes * cells, 9 * channels), bf16)],
        compiler_params=pltpu.CompilerParams(vmem_limit_bytes=16 * 1024 * 1024),
        cost_estimate=pl.CostEstimate(
            flops=2 * planes * cells * channels * (27 * channels + width),
            bytes_accessed=2_000_000, transcendentals=0,
        ),
        name="features_and_input_grad",
    )(hg, hg_low, hg_high, conv_weight.reshape(9, 3 * channels, channels), hidden, mix_weight)

    radices = [radix for _, _, radix in stages]
    if aligned:
        held = grads.reshape(radices + [piece, channels])
    else:
        flat = grads.reshape(-1)
        flat = jnp.pad(flat, (0, share * devices - flat.size))
        held = flat.reshape(dp_digits[::-1] + space_digits[::-1] + [share])
        count = len(radices)
        places = {}
        for spot, stage in enumerate(stages_of("dp", dp_digits)[::-1] + stages_of("space", space_digits)[::-1]):
            places[stage] = spot
            mine = lax.rem(lax.axis_index(stage[0]) // stage[1], stage[2])
            held = jnp.roll(held, -mine, axis=spot)
        held = jnp.transpose(held, [places[stage] for stage in stages] + [count])
    for axis, stride, radix in stages:
        size = lax.axis_size(axis)
        total = held[0].astype(f32)
        arrived = [lax.ppermute(held[k], axis, turned(size, stride, radix, k)) for k in range(1, radix)]
        for term in arrived:
            total = total + term.astype(f32)
        held = total.astype(bf16)
    weight_grads = (total / devices).reshape(-1)
    return (features.reshape(feature_grad.shape), input_grad.reshape(universes.shape), weight_grads)


def solution(mesh):
    return jax.shard_map(
        shards,
        mesh=mesh,
        in_specs=(P("dp", "space", None, None, None), P(), P(), P("dp", "space", None, None, None)),
        out_specs=(
            P("dp", "space", None, None, None),
            P("dp", "space", None, None, None),
            P(("dp", "space")),
        ),
        check_vma=False,
    )
```

```python
import functools

import jax
import jax.numpy as jnp
from jax import lax
from jax.experimental import pallas as pl
from jax.experimental.pallas import tpu as pltpu
from jax.sharding import PartitionSpec as P

leak_slope = 0.3
bf16 = jnp.bfloat16
f32 = jnp.float32
NT = (((1,), (1,)), ((), ()))
TN = (((0,), (0,)), ((), ()))
VMEM = pl.BlockSpec(memory_space=pltpu.VMEM)
HBM = pl.BlockSpec(memory_space=pltpu.HBM)


def shift_columns(value, step, columns):
    rows = value.shape[0]
    place = lax.rem(lax.broadcasted_iota(jnp.int32, value.shape, 0), columns)
    moved = pltpu.roll(value, step % rows, 0)
    edge = 0 if step == 1 else columns - 1
    return jnp.where(place == edge, 0.0, moved)


def gather_rows(target, row_start, column_start, source, row_shift, columns):
    cells, width = source.shape
    lanes = pl.ds(column_start, width)
    if row_shift == 0:
        target[pl.ds(row_start, cells), lanes] = source[...]
    elif row_shift < 0:
        target[pl.ds(row_start, columns), lanes] = jnp.zeros((columns, width), source.dtype)
        target[pl.ds(row_start + columns, cells - columns), lanes] = source[pl.ds(0, cells - columns), :]
    else:
        target[pl.ds(row_start, cells - columns), lanes] = source[pl.ds(columns, cells - columns), :]
        target[pl.ds(row_start + cells - columns, columns), lanes] = jnp.zeros((columns, width), source.dtype)


def beside(parity, pair_ref, cross_ref, place):
    @pl.when(parity == 0)
    def _():
        place(cross_ref.at[cross_ref.shape[0] - 1], pair_ref.at[0])

    @pl.when(parity == 1)
    def _():
        place(pair_ref.at[pair_ref.shape[0] - 1], cross_ref.at[0])


def join_columns(parts, step, columns):
    channels = parts.shape[1] // 3
    return (
        parts[:, channels : 2 * channels]
        + shift_columns(parts[:, :channels], step, columns)
        + shift_columns(parts[:, 2 * channels :], -step, columns)
    )


def inner_kernel(columns, x_hbm, w_hbm, mix_hbm, fg_hbm,
                 part_ref, pulled_ref, x_ref, wide, mix_ref, fg_ref, patch, sems):
    planes, cells, channels = x_ref.shape
    copies = [
        pltpu.make_async_copy(x_hbm, x_ref, sems.at[0]),
        pltpu.make_async_copy(fg_hbm, fg_ref, sems.at[1]),
        pltpu.make_async_copy(mix_hbm, mix_ref, sems.at[2]),
    ]
    for e in range(3):
        copies.append(pltpu.make_async_copy(
            w_hbm.at[:, e], wide.at[:, :, pl.ds(e * channels, channels)], sems.at[3 + e]
        ))
    for copy in copies:
        copy.start()
    copies[0].wait()
    for p in range(planes):
        for a in range(3):
            if 0 <= p + a - 1 < planes:
                for b in range(3):
                    gather_rows(
                        patch, p * cells, (a * 3 + b) * channels, x_ref.at[p + a - 1], b - 1, columns
                    )
    for copy in copies[1:3]:
        copy.wait()
    for p in range(planes):
        pulled_ref[p] = lax.dot_general(fg_ref[p], mix_ref[...], NT, preferred_element_type=f32)
    for copy in copies[3:]:
        copy.wait()
    for p in range(planes):
        first = 3 if p == 0 else 0
        last = 6 if p == planes - 1 else 9
        parts = jnp.dot(
            patch[pl.ds(p * cells, cells), pl.ds(first * channels, (last - first) * channels)],
            wide[first:last].reshape((last - first) * channels, 3 * channels),
            preferred_element_type=f32,
        )
        part_ref[p] = join_columns(parts, 1, columns)


def forward_kernel(columns, order, x_ref, pair_ref, cross_ref, wide, mix_ref, fg_ref, part_ref, pulled_ref,
                   hidden_ref, hg_ref, hg_pair_ref, hg_cross_ref, grads_ref, patch, cotangents, rows_ref):
    planes, cells, channels = x_ref.shape
    width = mix_ref.shape[1]
    parity = lax.rem(lax.axis_index("space"), 2)
    for p in range(planes):
        for a in range(3):
            if 0 <= p + a - 1 < planes:
                for b in range(3):
                    gather_rows(
                        patch, p * cells, (a * 3 + b) * channels, x_ref.at[p + a - 1], b - 1, columns
                    )

    def outer(low_ref, high_ref):
        for b in range(3):
            gather_rows(patch, 0, b * channels, low_ref, b - 1, columns)
            gather_rows(patch, (planes - 1) * cells, (6 + b) * channels, high_ref, b - 1, columns)

    beside(parity, pair_ref, cross_ref, outer)
    for p in range(planes):
        rows = pl.ds(p * cells, cells)
        summed = part_ref[p]
        for edge, first in ((0, 0), (planes - 1, 6)):
            if p == edge:
                parts = jnp.dot(
                    patch[rows, pl.ds(first * channels, 3 * channels)],
                    wide[first : first + 3].reshape(3 * channels, 3 * channels),
                    preferred_element_type=f32,
                )
                summed = summed + join_columns(parts, 1, columns)
        hidden_ref[p] = jnp.where(summed > 0, summed, leak_slope * summed).astype(bf16)
        hg = (pulled_ref[p] * jnp.where(summed > 0, 1.0, leak_slope)).astype(bf16)
        hg_ref[p] = hg
        wide_hg = hg.astype(f32)
        cotangents[rows, pl.ds(0, channels)] = shift_columns(wide_hg, -1, columns).astype(bf16)
        cotangents[rows, pl.ds(channels, channels)] = hg
        cotangents[rows, pl.ds(2 * channels, channels)] = shift_columns(wide_hg, 1, columns).astype(bf16)
    taps = 27 * channels
    mixed = jnp.zeros((channels, width), f32)
    for p in range(planes):
        mixed = mixed + lax.dot_general(hidden_ref[p], fg_ref[p], TN, preferred_element_type=f32)
    parts_of_mix = width // channels
    for j in range(parts_of_mix):
        rows_ref[pl.ds(taps + j, channels, stride=parts_of_mix), :] = mixed[:, j * channels : (j + 1) * channels]
    for ab in range(9):
        block = lax.dot_general(
            patch[:, pl.ds(ab * channels, channels)], cotangents[...], TN, preferred_element_type=f32
        )
        for e in range(3):
            rows_ref[pl.ds((ab * 3 + e) * channels, channels), :] = block[:, e * channels : (e + 1) * channels]
    if order is None:
        grads_ref[...] = rows_ref[...].astype(bf16)
    else:
        piece = grads_ref.shape[1]
        for k in range(grads_ref.shape[0]):
            grads_ref[order(k)] = rows_ref[pl.ds(k * piece, piece), :].astype(bf16)

    @pl.when(parity == 0)
    def _():
        hg_cross_ref[0] = hg_ref[0]
        hg_pair_ref[0] = hg_ref[planes - 1]

    @pl.when(parity == 1)
    def _():
        hg_cross_ref[0] = hg_ref[planes - 1]
        hg_pair_ref[0] = hg_ref[0]


def backward_kernel(columns, hg_ref, pair_ref, cross_ref, w_ref, hidden_ref, mix_ref,
                    features_ref, input_ref, patch):
    planes, cells, channels = hg_ref.shape
    for p in range(planes):
        features_ref[p] = jnp.dot(hidden_ref[p], mix_ref[...], preferred_element_type=f32).astype(bf16)
        for a in range(3):
            if 0 <= p + 1 - a < planes:
                for b in range(3):
                    gather_rows(
                        patch, p * cells, (a * 3 + b) * channels, hg_ref.at[p + 1 - a], 1 - b, columns
                    )

    def outer(low_ref, high_ref):
        for b in range(3):
            gather_rows(patch, 0, (6 + b) * channels, low_ref, 1 - b, columns)
            gather_rows(patch, (planes - 1) * cells, b * channels, high_ref, 1 - b, columns)

    beside(lax.rem(lax.axis_index("space"), 2), pair_ref, cross_ref, outer)
    for p in range(planes):
        parts = jnp.zeros((cells, 3 * channels), f32)
        for first in range(0, 9, 2):
            count = min(2, 9 - first)
            block = jnp.concatenate(
                [
                    jnp.concatenate(
                        [w_ref[first + i, :, e * channels : (e + 1) * channels] for e in range(3)], axis=0
                    )
                    for i in range(count)
                ],
                axis=1,
            )
            parts = parts + lax.dot_general(
                patch[pl.ds(p * cells, cells), pl.ds(first * channels, count * channels)],
                block, NT, preferred_element_type=f32,
            )
        input_ref[p] = join_columns(parts, -1, columns).astype(bf16)


def digits_of(count):
    digits = []
    while count > 1:
        for radix in (2, 3, 5, 7, count) if not digits else (4, 2, 3, 5, 7, count):
            if count % radix == 0:
                digits.append(radix)
                count //= radix
                break
    return digits


def stages_of(axis, digits):
    stages, stride = [], 1
    for radix in digits:
        stages.append((axis, stride, radix))
        stride *= radix
    return stages


def apart(digit, mine, radix):
    if radix & (radix - 1) == 0:
        return lax.bitwise_xor(mine, digit)
    return lax.rem(digit - mine + radix, radix)


def turned(count, stride, radix, k):
    pairs = []
    for i in range(count):
        digit = i // stride % radix
        other = digit ^ k if radix & (radix - 1) == 0 else (digit + k) % radix
        pairs.append((i, i + (other - digit) * stride))
    return pairs


def exchange(axis, for_pair, for_cross):
    count = lax.axis_size(axis)

    def swaps(start):
        found = []
        for i in range(start, count - 1, 2):
            found += [(i, i + 1), (i + 1, i)]
        return found

    cross = lax.ppermute(for_cross, axis, swaps(1))
    pair = lax.ppermute(for_pair, axis, swaps(0))
    return pair, cross


def shards(universes, conv_weight, mix_weight, feature_grad):
    channels = conv_weight.shape[1]
    width = mix_weight.shape[1]
    planes, map_rows, columns = universes.shape[1:4]
    cells = map_rows * columns
    group_count, slab_count = lax.axis_size("dp"), lax.axis_size("space")
    devices = group_count * slab_count
    space_digits = digits_of(slab_count)
    dp_digits = [4] if group_count == 4 else digits_of(group_count)
    stages = stages_of("space", space_digits) + stages_of("dp", dp_digits)

    x = universes.reshape(planes, cells, channels)
    fg = feature_grad.reshape(planes, cells, width)
    weights = conv_weight.reshape(9, 3, channels, channels)
    x_pair, x_cross = exchange("space", x, x)

    total_rows = 27 * channels + channels * width // channels
    share = (total_rows * channels + devices - 1) // devices
    aligned = share * devices == total_rows * channels and share % channels == 0
    if aligned:
        piece = share // channels
        grads_shape = (devices, piece, channels)

        def order(k):
            place = 0
            for axis, stride, radix in stages:
                index = k % slab_count if axis == "space" else k // slab_count
                mine = lax.rem(lax.axis_index(axis) // stride, radix)
                place = place * radix + apart(index // stride % radix, mine, radix)
            return place
    else:
        grads_shape = (total_rows, channels)
        order = None

    slab = jax.ShapeDtypeStruct((planes, cells, channels), bf16)
    slab_sum = jax.ShapeDtypeStruct((planes, cells, channels), f32)
    edge = jax.ShapeDtypeStruct((1, cells, channels), bf16)
    macs = planes * cells * channels * channels
    part, pulled, x_near, wide, mix_near, fg_near = pl.pallas_call(
        functools.partial(inner_kernel, columns),
        out_shape=(
            slab_sum,
            slab_sum,
            slab,
            jax.ShapeDtypeStruct((9, channels, 3 * channels), bf16),
            jax.ShapeDtypeStruct(mix_weight.shape, bf16),
            jax.ShapeDtypeStruct(fg.shape, bf16),
        ),
        in_specs=[HBM] * 4,
        out_specs=(VMEM,) * 6,
        scratch_shapes=[
            pltpu.VMEM((planes * cells, 9 * channels), bf16),
            pltpu.SemaphoreType.DMA((6,)),
        ],
        compiler_params=pltpu.CompilerParams(vmem_limit_bytes=16 * 1024 * 1024),
        cost_estimate=pl.CostEstimate(flops=2 * macs * 22, bytes_accessed=2_000_000, transcendentals=0),
        name="inner_taps",
    )(x, weights, mix_weight, fg)
    hidden, hg, hg_for_pair, hg_for_cross, grads = pl.pallas_call(
        functools.partial(forward_kernel, columns, order),
        out_shape=(slab, slab, edge, edge, jax.ShapeDtypeStruct(grads_shape, bf16)),
        in_specs=[VMEM] * 8,
        out_specs=(VMEM,) * 5,
        scratch_shapes=[
            pltpu.VMEM((planes * cells, 9 * channels), bf16),
            pltpu.VMEM((planes * cells, 3 * channels), bf16),
            pltpu.VMEM((total_rows, channels), f32),
        ],
        compiler_params=pltpu.CompilerParams(vmem_limit_bytes=16 * 1024 * 1024),
        cost_estimate=pl.CostEstimate(flops=2 * macs * 40, bytes_accessed=3_000_000, transcendentals=0),
        name="forward_and_kernel_grads",
    )(x_near, x_pair, x_cross, wide, mix_near, fg_near, part, pulled)

    hg_pair, hg_cross = exchange("space", hg_for_pair, hg_for_cross)
    features, input_grad = pl.pallas_call(
        functools.partial(backward_kernel, columns),
        out_shape=(jax.ShapeDtypeStruct((planes, cells, width), bf16), slab),
        in_specs=[VMEM] * 6,
        out_specs=(VMEM, VMEM),
        scratch_shapes=[pltpu.VMEM((planes * cells, 9 * channels), bf16)],
        compiler_params=pltpu.CompilerParams(vmem_limit_bytes=16 * 1024 * 1024),
        cost_estimate=pl.CostEstimate(flops=2 * macs * 29, bytes_accessed=2_000_000, transcendentals=0),
        name="features_and_input_grad",
    )(hg, hg_pair, hg_cross, wide, hidden, mix_near)

    radices = [radix for _, _, radix in stages]
    if aligned:
        held = grads.reshape(radices + [piece, channels])
    else:
        flat = grads.reshape(-1)
        flat = jnp.pad(flat, (0, share * devices - flat.size))
        held = flat.reshape(dp_digits[::-1] + space_digits[::-1] + [share])
        count = len(radices)
        places = {}
        for spot, stage in enumerate(stages_of("dp", dp_digits)[::-1] + stages_of("space", space_digits)[::-1]):
            places[stage] = spot
            mine = lax.rem(lax.axis_index(stage[0]) // stage[1], stage[2])
            held = jnp.take(held, apart(jnp.arange(stage[2]), mine, stage[2]), axis=spot)
        held = jnp.transpose(held, [places[stage] for stage in stages] + [count])
    for place, (axis, stride, radix) in enumerate(stages):
        size = lax.axis_size(axis)
        if place == 0 and len(radices) > 1:
            after = radices[1]
            arrived = [None] * after
            for far in range(after - 1, -1, -1):
                arrived[far] = [
                    lax.ppermute(held[k, far], axis, turned(size, stride, radix, k)) for k in range(1, radix)
                ]
            total = []
            for far in range(after):
                term = held[0, far].astype(f32)
                for other in arrived[far]:
                    term = term + other.astype(f32)
                total.append(term)
            held = [term.astype(bf16) for term in total]
            continue
        total = held[0].astype(f32)
        arrived = [lax.ppermute(held[k], axis, turned(size, stride, radix, k)) for k in range(radix - 1, 0, -1)]
        for term in arrived:
            total = total + term.astype(f32)
        held = total.astype(bf16)
    weight_grads = (total / devices).reshape(-1)
    return (features.reshape(feature_grad.shape), input_grad.reshape(universes.shape), weight_grads)


def solution(mesh):
    return jax.shard_map(
        shards,
        mesh=mesh,
        in_specs=(P("dp", "space", None, None, None), P(), P(), P("dp", "space", None, None, None)),
        out_specs=(
            P("dp", "space", None, None, None),
            P("dp", "space", None, None, None),
            P(("dp", "space")),
        ),
        check_vma=False,
    )
```

```python
import functools

import jax
import jax.numpy as jnp
from jax import lax
from jax.experimental import pallas as pl
from jax.experimental.pallas import tpu as pltpu
from jax.sharding import PartitionSpec as P

leak_slope = 0.3
bf16 = jnp.bfloat16
f32 = jnp.float32
NT = (((1,), (1,)), ((), ()))
TN = (((0,), (0,)), ((), ()))
VMEM = pl.BlockSpec(memory_space=pltpu.VMEM)
HBM = pl.BlockSpec(memory_space=pltpu.HBM)


def turn():
    parity = lax.rem(lax.axis_index("space"), 2)
    return parity, 2 * parity


def columns_kernel(columns, place_ref):
    place_ref[...] = lax.rem(lax.broadcasted_iota(jnp.int32, place_ref.shape, 0), columns)


def shift_columns(value, step, columns, place):
    moved = pltpu.roll(value, step % value.shape[0], 0)
    return jnp.where(place == (0 if step == 1 else columns - 1), 0.0, moved)


def join_columns(parts, step, columns, place):
    channels = parts.shape[1] // 3
    return (
        parts[:, channels : 2 * channels]
        + shift_columns(parts[:, :channels], step, columns, place)
        + shift_columns(parts[:, 2 * channels :], -step, columns, place)
    )


def spread_columns(hg, columns, place):
    value = hg.astype(f32)
    return jnp.concatenate(
        [
            shift_columns(value, -1, columns, place).astype(bf16),
            hg,
            shift_columns(value, 1, columns, place).astype(bf16),
        ],
        axis=1,
    )


def fill_rows(patch, a, plane, columns, mirror):
    cells, channels = plane.shape
    edge = jnp.zeros((columns, channels), plane.dtype)
    for b in range(3):
        at = a * 3 + b
        step = 1 - b if mirror else b - 1
        if step == 0:
            patch[at] = plane[...]
        elif step < 0:
            patch[at, pl.ds(0, columns), :] = edge
            patch[at, pl.ds(columns, cells - columns), :] = plane[pl.ds(0, cells - columns), :]
        else:
            patch[at, pl.ds(0, cells - columns), :] = plane[pl.ds(columns, cells - columns), :]
            patch[at, pl.ds(cells - columns, columns), :] = edge


def taps_dot(patch, wide, taps):
    return jnp.dot(
        jnp.concatenate([patch[t] for t in taps], axis=1),
        jnp.concatenate([wide[t] for t in taps], axis=0),
        preferred_element_type=f32,
    )


def clear_outside(patch, a):
    index = lax.axis_index("space")

    @pl.when(jnp.logical_or(index == 0, index == lax.axis_size("space") - 1))
    def _():
        for b in range(3):
            patch[a * 3 + b] = jnp.zeros(patch.shape[1:], patch.dtype)


def activate(summed, pulled, hidden_ref, hg_ref):
    hidden_ref[0] = jnp.where(summed > 0, summed, leak_slope * summed).astype(bf16)
    hg_ref[0] = (pulled * jnp.where(summed > 0, 1.0, leak_slope)).astype(bf16)


def kernel_grads(columns, place, patch, hidden_ref, hg_ref, fg, rows_ref, before_ref):
    channels = hidden_ref.shape[2]
    width = fg.shape[1]
    wide_hg = spread_columns(hg_ref[0], columns, place)
    for ab in range(9):
        block = lax.dot_general(patch[ab], wide_hg, TN, preferred_element_type=f32)
        for e in range(3):
            rows = pl.ds((ab * 3 + e) * channels, channels)
            value = block[:, e * channels : (e + 1) * channels]
            rows_ref[rows, :] = value if before_ref is None else value + before_ref[rows, :]
    mixed = lax.dot_general(hidden_ref[0], fg, TN, preferred_element_type=f32)
    parts = width // channels
    for j in range(parts):
        rows = pl.ds(27 * channels + j, channels, stride=parts)
        value = mixed[:, j * channels : (j + 1) * channels]
        rows_ref[rows, :] = value if before_ref is None else value + before_ref[rows, :]


def inner_kernel(columns, place_ref, w_hbm, mix_hbm, fg_hbm, near_ref, far_ref,
                 near_part, far_part, near_pulled, far_pulled, wide, mix_ref, fg_ref,
                 near_patch, far_patch, sems):
    channels = near_ref.shape[2]
    parity, side = turn()
    copies = [
        pltpu.make_async_copy(fg_hbm, fg_ref, sems.at[0]),
        pltpu.make_async_copy(mix_hbm, mix_ref, sems.at[1]),
    ]
    for e in range(3):
        copies.append(pltpu.make_async_copy(
            w_hbm.at[:, e], wide.at[:, :, pl.ds(e * channels, channels)], sems.at[2 + e]
        ))
    for copy in copies:
        copy.start()
    fill_rows(near_patch, 1, near_ref.at[0], columns, False)
    fill_rows(near_patch, side, far_ref.at[0], columns, False)
    fill_rows(far_patch, 1, far_ref.at[0], columns, False)
    fill_rows(far_patch, 2 - side, near_ref.at[0], columns, False)
    for copy in copies[:2]:
        copy.wait()
    near_pulled[...] = lax.dot_general(fg_ref[1 - parity], mix_ref[...], NT, preferred_element_type=f32)
    far_pulled[...] = lax.dot_general(fg_ref[parity], mix_ref[...], NT, preferred_element_type=f32)
    for copy in copies[2:]:
        copy.wait()
    for part, patch, a in ((near_part, near_patch, side), (far_part, far_patch, 2 - side)):
        taps = [3, 4, 5] + [a * 3 + b for b in range(3)]
        part[...] = join_columns(taps_dot(patch, wide, taps), 1, columns, place_ref[...])


def finish_plane(columns, place, patch, a, wide, part_ref, pulled_ref, fg, before_ref, hidden_ref, hg_ref, rows_ref):
    taps = [a * 3 + b for b in range(3)]
    summed = part_ref[...] + join_columns(taps_dot(patch, wide, taps), 1, columns, place)
    activate(summed, pulled_ref[...], hidden_ref, hg_ref)
    kernel_grads(columns, place, patch, hidden_ref, hg_ref, fg, rows_ref, before_ref)


def near_kernel(columns, place_ref, near_ref, far_ref, pair_ref, wide, fg_ref, part_ref, pulled_ref,
                hidden_ref, hg_ref, rows_ref, patch):
    parity, side = turn()
    fill_rows(patch, 2 - side, pair_ref.at[0], columns, False)
    fill_rows(patch, 1, near_ref.at[0], columns, False)
    fill_rows(patch, side, far_ref.at[0], columns, False)
    finish_plane(columns, place_ref[...], patch, 2 - side, wide, part_ref, pulled_ref, fg_ref[1 - parity], None,
                 hidden_ref, hg_ref, rows_ref)


def far_kernel(columns, order, place_ref, near_ref, far_ref, cross_ref, wide, fg_ref, part_ref, pulled_ref, before_ref,
               near_hg,
               hidden_ref, hg_ref, grads_ref, patch, rows_ref):
    parity, side = turn()
    fill_rows(patch, side, cross_ref.at[0], columns, False)
    clear_outside(patch, side)
    fill_rows(patch, 1, far_ref.at[0], columns, False)
    fill_rows(patch, 2 - side, near_ref.at[0], columns, False)
    finish_plane(columns, place_ref[...], patch, side, wide, part_ref, pulled_ref, fg_ref[parity], before_ref,
                 hidden_ref, hg_ref, rows_ref)
    if order is None:
        grads_ref[...] = rows_ref[...].astype(bf16)
    else:
        piece = grads_ref.shape[1]
        spots = order()
        for k, spot in enumerate(spots):
            grads_ref[spot] = rows_ref[pl.ds(k * piece, piece), :].astype(bf16)
        for spot, first, rows in runs_of(near_hg.shape[1], piece):
            grads_ref[len(spots) + spot, pl.ds(0, rows), :] = near_hg[0, pl.ds(first, rows), :]


def runs_of(cells, piece):
    step = piece // 16 * 16
    return [(spot, first, min(step, cells - first)) for spot, first in enumerate(range(0, cells, step))]


def split_kernel(start, kept_ref, came_ref, after_ref, own_ref, *out_refs):
    lot = own_ref.shape[0]
    for chip in range(len(out_refs) + 1):
        for i in range(lot):
            at = chip * lot + i
            value = kept_ref[start + at].astype(f32) + came_ref[at].astype(f32)
            if chip == 0:
                own_ref[i] = value
            else:
                out_refs[chip - 1][i] = value.astype(bf16)


def gather_kernel(keeps, own_ref, *refs):
    lot = own_ref.shape[0]
    came, out = refs[: len(refs) - lot], refs[len(refs) - lot :]
    for i in range(lot):
        value = own_ref[i]
        for ref in came:
            value = value + ref[i].astype(f32)
        out[i][...] = value if keeps and i == 0 else value.astype(bf16)


def backward_kernel(columns, place_ref, near_ref, far_ref, pair_ref, cross_ref, wide, mix_ref, near_hidden, far_hidden,
                    features_ref, input_ref, near_patch, far_patch, pair_plane):
    cells, channels = near_ref.shape[1:]
    if pair_ref.shape[1] == cells:
        pair_plane[...] = pair_ref[0]
    else:
        spots = runs_of(cells, pair_ref.shape[1])
        start = pair_ref.shape[0] - len(spots)
        for spot, first, rows in spots:
            pair_plane[pl.ds(first, rows), :] = pair_ref[start + spot, pl.ds(0, rows), :]
    parity, side = turn()
    features_ref[1 - parity] = jnp.dot(near_hidden[0], mix_ref[...], preferred_element_type=f32).astype(bf16)
    features_ref[parity] = jnp.dot(far_hidden[0], mix_ref[...], preferred_element_type=f32).astype(bf16)
    fill_rows(near_patch, side, pair_plane, columns, True)
    fill_rows(near_patch, 1, near_ref.at[0], columns, True)
    fill_rows(near_patch, 2 - side, far_ref.at[0], columns, True)
    fill_rows(far_patch, side, near_ref.at[0], columns, True)
    fill_rows(far_patch, 1, far_ref.at[0], columns, True)
    fill_rows(far_patch, 2 - side, cross_ref.at[0], columns, True)
    clear_outside(far_patch, 2 - side)
    for patch, plane in ((near_patch, 1 - parity), (far_patch, parity)):
        parts = jnp.zeros((near_ref.shape[1], 3 * channels), f32)
        for first in range(0, 9, 2):
            taps = range(first, min(first + 2, 9))
            block = jnp.concatenate(
                [
                    jnp.concatenate([wide[t, :, e * channels : (e + 1) * channels] for e in range(3)], axis=0)
                    for t in taps
                ],
                axis=1,
            )
            parts = parts + lax.dot_general(
                jnp.concatenate([patch[t] for t in taps], axis=1), block, NT, preferred_element_type=f32
            )
        input_ref[plane] = join_columns(parts, -1, columns, place_ref[...]).astype(bf16)


def digits_of(count):
    digits = []
    while count > 1:
        for radix in (2, 3, 5, 7, count) if not digits else (4, 2, 3, 5, 7, count):
            if count % radix == 0:
                digits.append(radix)
                count //= radix
                break
    return digits


def stages_of(axis, digits):
    stages, stride = [], 1
    for radix in digits:
        stages.append((axis, stride, radix))
        stride *= radix
    return stages


def apart(digit, mine, radix):
    if radix & (radix - 1) == 0:
        return lax.bitwise_xor(mine, digit)
    return lax.rem(digit - mine + radix, radix)


def send(value, stage, k):
    axis, stride, radix = stage
    pairs = []
    for i in range(lax.axis_size(axis)):
        digit = i // stride % radix
        other = digit ^ k if radix & (radix - 1) == 0 else (digit + k) % radix
        pairs.append((i, i + (other - digit) * stride))
    return lax.ppermute(value, axis, pairs)


def swaps(start, count):
    found = []
    for i in range(start, count + start, 2):
        found += [(i, (i + 1) % count), ((i + 1) % count, i)]
    return found


def shards(universes, conv_weight, mix_weight, feature_grad):
    channels = conv_weight.shape[1]
    width = mix_weight.shape[1]
    planes, map_rows, columns = universes.shape[1:4]
    if planes != 2 or lax.axis_size("space") % 2:
        raise ValueError("slab shape")
    cells = map_rows * columns
    group_count, slab_count = lax.axis_size("dp"), lax.axis_size("space")
    devices = group_count * slab_count
    space_digits = digits_of(slab_count)
    dp_digits = [4] if group_count == 4 else digits_of(group_count)
    stages = stages_of("space", space_digits) + stages_of("dp", dp_digits)

    x = universes.reshape(planes, cells, channels)
    fg = feature_grad.reshape(planes, cells, width)
    weights = conv_weight.reshape(9, 3, channels, channels)
    pair_swaps, cross_swaps = swaps(0, slab_count), swaps(1, slab_count)

    parity = lax.rem(lax.axis_index("space"), 2)
    x_near = lax.dynamic_slice_in_dim(x, 1 - parity, 1, 0)
    x_far = lax.dynamic_slice_in_dim(x, parity, 1, 0)
    x_cross = lax.ppermute(x_far, "space", cross_swaps)
    x_pair = lax.ppermute(x_near, "space", pair_swaps)

    total_rows = 27 * channels + channels * width // channels
    share = (total_rows * channels + devices - 1) // devices
    lots = (
        share * devices == total_rows * channels
        and share % channels == 0
        and len(stages) == 3
        and stages[0][2] == 2
        and stages[2][2] % 2 == 0
    )
    if lots:
        piece = share // channels
        chips, groups = stages[1][2], stages[2][2]
        lot = groups // 2
        grads_shape = (devices + len(runs_of(cells, piece)), piece, channels)

        def order():
            def relative(stage):
                axis, stride, radix = stage
                mine = lax.rem(lax.div(lax.axis_index(axis), stride), radix)
                return [apart(digit, mine, radix) for digit in range(radix)]

            cores = [core * (2 * chips * lot) for core in relative(stages[0])]
            chip_spots = [chip * lot for chip in relative(stages[1])]
            group_spots = [
                (1 - lax.div(group, lot)) * (chips * lot) + lax.rem(group, lot) for group in relative(stages[2])
            ]
            spots = []
            for k in range(devices):
                group, place = divmod(k, slab_count)
                chip, core = divmod(place, 2)
                spots.append(cores[core] + chip_spots[chip] + group_spots[group])
            return spots
    else:
        grads_shape = (total_rows, channels)
        order = None

    def like(*shape, dtype=bf16):
        return jax.ShapeDtypeStruct(shape, dtype)

    def params(mebibytes):
        return pltpu.CompilerParams(vmem_limit_bytes=mebibytes * 1024 * 1024)

    def cost(blocks, read):
        return pl.CostEstimate(
            flops=2 * cells * channels * channels * blocks, bytes_accessed=read, transcendentals=0
        )

    plane = like(1, cells, channels)
    plane_sum = like(cells, channels, dtype=f32)
    patch = pltpu.VMEM((9, cells, channels), bf16)
    place = pl.pallas_call(
        functools.partial(columns_kernel, columns),
        out_shape=like(cells, channels, dtype=jnp.int32),
        out_specs=VMEM,
        compiler_params=params(4),
        cost_estimate=cost(100, 8_000_000),
        name="columns_of_cells",
    )()
    near_part, far_part, near_pulled, far_pulled, wide, mix_near, fg_near = pl.pallas_call(
        functools.partial(inner_kernel, columns),
        out_shape=(plane_sum,) * 4
        + (like(9, channels, 3 * channels), like(*mix_weight.shape), like(*fg.shape)),
        in_specs=[VMEM] + [HBM] * 3 + [VMEM] * 2,
        out_specs=(VMEM,) * 7,
        scratch_shapes=[patch, patch, pltpu.SemaphoreType.DMA((5,))],
        compiler_params=params(16),
        cost_estimate=cost(44, 2_000_000),
        name="inner_taps",
    )(place, weights, mix_weight, fg, x_near, x_far)
    near_hidden, near_hg, near_rows = pl.pallas_call(
        functools.partial(near_kernel, columns),
        out_shape=(plane, plane, like(total_rows, channels, dtype=f32)),
        in_specs=[VMEM] * 8,
        out_specs=(VMEM,) * 3,
        scratch_shapes=[patch],
        compiler_params=params(16),
        cost_estimate=cost(38, 3_000_000),
        name="near_plane",
    )(place, x_near, x_far, x_pair, wide, fg_near, near_part, near_pulled)
    far_hidden, far_hg, grads = pl.pallas_call(
        functools.partial(far_kernel, columns, order),
        out_shape=(plane, plane, like(*grads_shape)),
        in_specs=[VMEM] * 10,
        out_specs=(VMEM,) * 3,
        scratch_shapes=[patch, pltpu.VMEM((total_rows, channels), f32)],
        compiler_params=params(16),
        cost_estimate=cost(38, 3_000_000),
        name="far_plane",
    )(place, x_near, x_far, x_cross, wide, fg_near, far_part, far_pulled, near_rows, near_hg)

    hg_cross = lax.ppermute(far_hg, "space", cross_swaps)
    if lots:
        size = devices // 4
        first = send(grads[2 * size : 3 * size], stages[0], 1)
        second = send(grads[3 * size :], stages[0], 1)
        hg_pair = second
    else:
        hg_pair = lax.ppermute(near_hg, "space", pair_swaps)
    features, input_grad = pl.pallas_call(
        functools.partial(backward_kernel, columns),
        out_shape=(like(planes, cells, width), like(planes, cells, channels)),
        in_specs=[VMEM] * 9,
        out_specs=(VMEM, VMEM),
        scratch_shapes=[patch, patch, pltpu.VMEM((cells, channels), bf16)],
        compiler_params=params(16),
        cost_estimate=cost(58, 2_000_000),
        name="features_and_input_grad",
    )(place, near_hg, far_hg, hg_pair, hg_cross, wide, mix_near, near_hidden, far_hidden)

    if lots:
        arrived = []
        for start, came, near in ((0, first, False), (size, second, True)):
            own, *others = pl.pallas_call(
                functools.partial(split_kernel, start),
                out_shape=[like(lot, piece, channels, dtype=f32)] + [like(lot, piece, channels)] * (chips - 1),
                in_specs=[VMEM, VMEM, pl.BlockSpec(memory_space=pl.ANY)],
                out_specs=[VMEM] * chips,
                compiler_params=params(8),
                name="sum_of_core_pair",
            )(grads, came, hg_cross if near else came)
            came = [send(others[k - 1], stages[1], k) for k in range(1, chips)]
            parts = pl.pallas_call(
                functools.partial(gather_kernel, near),
                out_shape=[like(piece, channels, dtype=f32 if near and i == 0 else bf16) for i in range(lot)],
                in_specs=[VMEM] * chips,
                out_specs=[VMEM] * lot,
                compiler_params=params(8),
                name="sum_of_chips",
            )(own, *came)
            for i in range(lot):
                k = i if near else lot + i
                arrived.append(send(parts[i], stages[2], k).astype(f32) if k else parts[i])
        total = sum(arrived[1:], arrived[0])
    else:
        flat = grads.reshape(-1)
        flat = jnp.pad(flat, (0, share * devices - flat.size))
        held = flat.reshape(dp_digits[::-1] + space_digits[::-1] + [share])
        places = {}
        for spot, stage in enumerate(stages_of("dp", dp_digits)[::-1] + stages_of("space", space_digits)[::-1]):
            places[stage] = spot
            mine = lax.rem(lax.axis_index(stage[0]) // stage[1], stage[2])
            held = jnp.take(held, apart(jnp.arange(stage[2]), mine, stage[2]), axis=spot)
        parts = jnp.transpose(held, [places[stage] for stage in stages] + [len(stages)])
        for stage in stages:
            total = parts[0].astype(f32)
            for term in [send(parts[k], stage, k) for k in range(1, stage[2])]:
                total = total + term.astype(f32)
            parts = total.astype(bf16)
    weight_grads = (total / devices).reshape(-1)
    return (features.reshape(feature_grad.shape), input_grad.reshape(universes.shape), weight_grads)


def solution(mesh):
    return jax.shard_map(
        shards,
        mesh=mesh,
        in_specs=(P("dp", "space", None, None, None), P(), P(), P("dp", "space", None, None, None)),
        out_specs=(
            P("dp", "space", None, None, None),
            P("dp", "space", None, None, None),
            P(("dp", "space")),
        ),
        check_vma=False,
    )
```

```python
import functools

import jax
import jax.numpy as jnp
from jax import lax
from jax.experimental import pallas as pl
from jax.experimental.pallas import tpu as pltpu
from jax.sharding import PartitionSpec as P

leak_slope = 0.3
bf16 = jnp.bfloat16
f32 = jnp.float32
NT = (((1,), (1,)), ((), ()))
TN = (((0,), (0,)), ((), ()))
VMEM = pl.BlockSpec(memory_space=pltpu.VMEM)
HBM = pl.BlockSpec(memory_space=pltpu.HBM)


def turn():
    parity = lax.rem(lax.axis_index("space"), 2)
    return parity, 2 * parity


def columns_kernel(columns, place_ref):
    place_ref[...] = lax.rem(lax.broadcasted_iota(jnp.int32, place_ref.shape, 0), columns)


def shift_columns(value, step, columns, place):
    moved = pltpu.roll(value, step % value.shape[0], 0)
    return jnp.where(place == (0 if step == 1 else columns - 1), 0.0, moved)


def join_columns(parts, step, columns, place):
    channels = parts.shape[1] // 3
    return (
        parts[:, channels : 2 * channels]
        + shift_columns(parts[:, :channels], step, columns, place)
        + shift_columns(parts[:, 2 * channels :], -step, columns, place)
    )


def spread_columns(hg, columns, place):
    value = hg.astype(f32)
    return jnp.concatenate(
        [
            shift_columns(value, -1, columns, place).astype(bf16),
            hg,
            shift_columns(value, 1, columns, place).astype(bf16),
        ],
        axis=1,
    )


def fill_rows(patch, a, plane, columns, mirror):
    cells, channels = plane.shape
    edge = jnp.zeros((columns, channels), plane.dtype)
    for b in range(3):
        at = a * 3 + b
        step = 1 - b if mirror else b - 1
        if step == 0:
            patch[at] = plane[...]
        elif step < 0:
            patch[at, pl.ds(0, columns), :] = edge
            patch[at, pl.ds(columns, cells - columns), :] = plane[pl.ds(0, cells - columns), :]
        else:
            patch[at, pl.ds(0, cells - columns), :] = plane[pl.ds(columns, cells - columns), :]
            patch[at, pl.ds(cells - columns, columns), :] = edge


def taps_dot(patch, wide, taps):
    return jnp.dot(
        jnp.concatenate([patch[t] for t in taps], axis=1),
        jnp.concatenate([wide[t] for t in taps], axis=0),
        preferred_element_type=f32,
    )


def clear_outside(patch, a):
    index = lax.axis_index("space")

    @pl.when(jnp.logical_or(index == 0, index == lax.axis_size("space") - 1))
    def _():
        for b in range(3):
            patch[a * 3 + b] = jnp.zeros(patch.shape[1:], patch.dtype)


def activate(summed, pulled, hidden_ref, hg_ref):
    hidden_ref[0] = jnp.where(summed > 0, summed, leak_slope * summed).astype(bf16)
    hg_ref[0] = (pulled * jnp.where(summed > 0, 1.0, leak_slope)).astype(bf16)


def kernel_grads(columns, place, patch, hidden_ref, hg_ref, fg, rows_ref, before_ref):
    channels = hidden_ref.shape[2]
    width = fg.shape[1]
    wide_hg = spread_columns(hg_ref[0], columns, place)
    for ab in range(9):
        block = lax.dot_general(patch[ab], wide_hg, TN, preferred_element_type=f32)
        for e in range(3):
            rows = pl.ds((ab * 3 + e) * channels, channels)
            value = block[:, e * channels : (e + 1) * channels]
            rows_ref[rows, :] = value if before_ref is None else value + before_ref[rows, :]
    mixed = lax.dot_general(hidden_ref[0], fg, TN, preferred_element_type=f32)
    parts = width // channels
    for j in range(parts):
        rows = pl.ds(27 * channels + j, channels, stride=parts)
        value = mixed[:, j * channels : (j + 1) * channels]
        rows_ref[rows, :] = value if before_ref is None else value + before_ref[rows, :]


def inner_kernel(columns, place_ref, w_hbm, mix_hbm, fg_hbm, near_ref, far_ref,
                 near_part, far_part, near_pulled, far_pulled, wide, mix_ref, fg_ref,
                 near_patch, far_patch, sems):
    channels = near_ref.shape[2]
    parity, side = turn()
    copies = [
        pltpu.make_async_copy(fg_hbm, fg_ref, sems.at[0]),
        pltpu.make_async_copy(mix_hbm, mix_ref, sems.at[1]),
    ]
    for e in range(3):
        copies.append(pltpu.make_async_copy(
            w_hbm.at[:, e], wide.at[:, :, pl.ds(e * channels, channels)], sems.at[2 + e]
        ))
    for copy in copies:
        copy.start()
    fill_rows(near_patch, 1, near_ref.at[0], columns, False)
    fill_rows(near_patch, side, far_ref.at[0], columns, False)
    fill_rows(far_patch, 1, far_ref.at[0], columns, False)
    fill_rows(far_patch, 2 - side, near_ref.at[0], columns, False)
    for copy in copies[:2]:
        copy.wait()
    near_pulled[...] = lax.dot_general(fg_ref[1 - parity], mix_ref[...], NT, preferred_element_type=f32)
    far_pulled[...] = lax.dot_general(fg_ref[parity], mix_ref[...], NT, preferred_element_type=f32)
    for copy in copies[2:]:
        copy.wait()
    for part, patch, a in ((near_part, near_patch, side), (far_part, far_patch, 2 - side)):
        taps = [3, 4, 5] + [a * 3 + b for b in range(3)]
        part[...] = join_columns(taps_dot(patch, wide, taps), 1, columns, place_ref[...])


def finish_plane(columns, place, patch, a, wide, part_ref, pulled_ref, fg, before_ref, hidden_ref, hg_ref, rows_ref):
    taps = [a * 3 + b for b in range(3)]
    summed = part_ref[...] + join_columns(taps_dot(patch, wide, taps), 1, columns, place)
    activate(summed, pulled_ref[...], hidden_ref, hg_ref)
    kernel_grads(columns, place, patch, hidden_ref, hg_ref, fg, rows_ref, before_ref)


def near_kernel(columns, place_ref, near_ref, far_ref, pair_ref, wide, fg_ref, part_ref, pulled_ref,
                hidden_ref, hg_ref, rows_ref, patch):
    parity, side = turn()
    fill_rows(patch, 2 - side, pair_ref.at[0], columns, False)
    fill_rows(patch, 1, near_ref.at[0], columns, False)
    fill_rows(patch, side, far_ref.at[0], columns, False)
    finish_plane(columns, place_ref[...], patch, 2 - side, wide, part_ref, pulled_ref, fg_ref[1 - parity], None,
                 hidden_ref, hg_ref, rows_ref)


def far_kernel(columns, order, place_ref, near_ref, far_ref, cross_ref, wide, fg_ref, part_ref, pulled_ref, before_ref,
               near_hg,
               hidden_ref, hg_ref, grads_ref, patch, rows_ref):
    parity, side = turn()
    fill_rows(patch, side, cross_ref.at[0], columns, False)
    clear_outside(patch, side)
    fill_rows(patch, 1, far_ref.at[0], columns, False)
    fill_rows(patch, 2 - side, near_ref.at[0], columns, False)
    finish_plane(columns, place_ref[...], patch, side, wide, part_ref, pulled_ref, fg_ref[parity], before_ref,
                 hidden_ref, hg_ref, rows_ref)
    if order is None:
        grads_ref[...] = rows_ref[...].astype(bf16)
    else:
        piece = grads_ref.shape[1]
        spots = order()
        for k, spot in enumerate(spots):
            grads_ref[spot] = rows_ref[pl.ds(k * piece, piece), :].astype(bf16)
        for spot, first, rows in runs_of(near_hg.shape[1], piece):
            grads_ref[len(spots) + spot, pl.ds(0, rows), :] = near_hg[0, pl.ds(first, rows), :]


def runs_of(cells, piece):
    step = piece // 16 * 16
    return [(spot, first, min(step, cells - first)) for spot, first in enumerate(range(0, cells, step))]


def split_kernel(start, kept_ref, came_ref, own_ref, *out_refs):
    lot = own_ref.shape[0]
    for chip in range(len(out_refs) + 1):
        for i in range(lot):
            at = chip * lot + i
            value = kept_ref[start + at].astype(f32) + came_ref[at].astype(f32)
            if chip == 0:
                own_ref[i] = value
            else:
                out_refs[chip - 1][i] = value.astype(bf16)


def gather_kernel(keeps, after_ref, own_ref, *refs):
    lot = own_ref.shape[0]
    came, out = refs[: len(refs) - lot], refs[len(refs) - lot :]
    for i in range(lot):
        value = own_ref[i]
        for ref in came:
            value = value + ref[i].astype(f32)
        out[i][...] = value if keeps and i == 0 else value.astype(bf16)


def backward_kernel(columns, place_ref, near_ref, far_ref, pair_ref, cross_ref, wide, mix_ref, near_hidden, far_hidden,
                    features_ref, input_ref, near_patch, far_patch, pair_plane):
    cells, channels = near_ref.shape[1:]
    if pair_ref.shape[1] == cells:
        pair_plane[...] = pair_ref[0]
    else:
        spots = runs_of(cells, pair_ref.shape[1])
        start = pair_ref.shape[0] - len(spots)
        for spot, first, rows in spots:
            pair_plane[pl.ds(first, rows), :] = pair_ref[start + spot, pl.ds(0, rows), :]
    parity, side = turn()
    features_ref[1 - parity] = jnp.dot(near_hidden[0], mix_ref[...], preferred_element_type=f32).astype(bf16)
    features_ref[parity] = jnp.dot(far_hidden[0], mix_ref[...], preferred_element_type=f32).astype(bf16)
    fill_rows(near_patch, side, pair_plane, columns, True)
    fill_rows(near_patch, 1, near_ref.at[0], columns, True)
    fill_rows(near_patch, 2 - side, far_ref.at[0], columns, True)
    fill_rows(far_patch, side, near_ref.at[0], columns, True)
    fill_rows(far_patch, 1, far_ref.at[0], columns, True)
    fill_rows(far_patch, 2 - side, cross_ref.at[0], columns, True)
    clear_outside(far_patch, 2 - side)
    for patch, plane in ((near_patch, 1 - parity), (far_patch, parity)):
        parts = jnp.zeros((near_ref.shape[1], 3 * channels), f32)
        for first in range(0, 9, 2):
            taps = range(first, min(first + 2, 9))
            block = jnp.concatenate(
                [
                    jnp.concatenate([wide[t, :, e * channels : (e + 1) * channels] for e in range(3)], axis=0)
                    for t in taps
                ],
                axis=1,
            )
            parts = parts + lax.dot_general(
                jnp.concatenate([patch[t] for t in taps], axis=1), block, NT, preferred_element_type=f32
            )
        input_ref[plane] = join_columns(parts, -1, columns, place_ref[...]).astype(bf16)


def digits_of(count):
    digits = []
    while count > 1:
        for radix in (2, 3, 5, 7, count) if not digits else (4, 2, 3, 5, 7, count):
            if count % radix == 0:
                digits.append(radix)
                count //= radix
                break
    return digits


def stages_of(axis, digits):
    stages, stride = [], 1
    for radix in digits:
        stages.append((axis, stride, radix))
        stride *= radix
    return stages


def apart(digit, mine, radix):
    if radix & (radix - 1) == 0:
        return lax.bitwise_xor(mine, digit)
    return lax.rem(digit - mine + radix, radix)


def send(value, stage, k):
    axis, stride, radix = stage
    pairs = []
    for i in range(lax.axis_size(axis)):
        digit = i // stride % radix
        other = digit ^ k if radix & (radix - 1) == 0 else (digit + k) % radix
        pairs.append((i, i + (other - digit) * stride))
    return lax.ppermute(value, axis, pairs)


def swaps(start, count):
    found = []
    for i in range(start, count + start, 2):
        found += [(i, (i + 1) % count), ((i + 1) % count, i)]
    return found


def shards(universes, conv_weight, mix_weight, feature_grad):
    channels = conv_weight.shape[1]
    width = mix_weight.shape[1]
    planes, map_rows, columns = universes.shape[1:4]
    if planes != 2 or lax.axis_size("space") % 2:
        raise ValueError("slab shape")
    cells = map_rows * columns
    group_count, slab_count = lax.axis_size("dp"), lax.axis_size("space")
    devices = group_count * slab_count
    space_digits = digits_of(slab_count)
    dp_digits = [4] if group_count == 4 else digits_of(group_count)
    stages = stages_of("space", space_digits) + stages_of("dp", dp_digits)

    x = universes.reshape(planes, cells, channels)
    fg = feature_grad.reshape(planes, cells, width)
    weights = conv_weight.reshape(9, 3, channels, channels)
    pair_swaps, cross_swaps = swaps(0, slab_count), swaps(1, slab_count)

    parity = lax.rem(lax.axis_index("space"), 2)
    x_near = lax.dynamic_slice_in_dim(x, 1 - parity, 1, 0)
    x_far = lax.dynamic_slice_in_dim(x, parity, 1, 0)
    x_cross = lax.ppermute(x_far, "space", cross_swaps)
    x_pair = lax.ppermute(x_near, "space", pair_swaps)

    total_rows = 27 * channels + channels * width // channels
    share = (total_rows * channels + devices - 1) // devices
    lots = (
        share * devices == total_rows * channels
        and share % channels == 0
        and len(stages) == 3
        and stages[0][2] == 2
        and stages[2][2] % 2 == 0
    )
    if lots:
        piece = share // channels
        chips, groups = stages[1][2], stages[2][2]
        lot = groups // 2
        grads_shape = (devices + len(runs_of(cells, piece)), piece, channels)

        def order():
            def relative(stage):
                axis, stride, radix = stage
                mine = lax.rem(lax.div(lax.axis_index(axis), stride), radix)
                return [apart(digit, mine, radix) for digit in range(radix)]

            cores = [core * (2 * chips * lot) for core in relative(stages[0])]
            chip_spots = [chip * lot for chip in relative(stages[1])]
            group_spots = [
                (1 - lax.div(group, lot)) * (chips * lot) + lax.rem(group, lot) for group in relative(stages[2])
            ]
            spots = []
            for k in range(devices):
                group, place = divmod(k, slab_count)
                chip, core = divmod(place, 2)
                spots.append(cores[core] + chip_spots[chip] + group_spots[group])
            return spots
    else:
        grads_shape = (total_rows, channels)
        order = None

    def like(*shape, dtype=bf16):
        return jax.ShapeDtypeStruct(shape, dtype)

    def params(mebibytes):
        return pltpu.CompilerParams(vmem_limit_bytes=mebibytes * 1024 * 1024)

    def cost(blocks, read):
        return pl.CostEstimate(
            flops=2 * cells * channels * channels * blocks, bytes_accessed=read, transcendentals=0
        )

    plane = like(1, cells, channels)
    plane_sum = like(cells, channels, dtype=f32)
    patch = pltpu.VMEM((9, cells, channels), bf16)
    place = pl.pallas_call(
        functools.partial(columns_kernel, columns),
        out_shape=like(cells, channels, dtype=jnp.int32),
        out_specs=VMEM,
        compiler_params=params(4),
        cost_estimate=cost(100, 8_000_000),
        name="columns_of_cells",
    )()
    near_part, far_part, near_pulled, far_pulled, wide, mix_near, fg_near = pl.pallas_call(
        functools.partial(inner_kernel, columns),
        out_shape=(plane_sum,) * 4
        + (like(9, channels, 3 * channels), like(*mix_weight.shape), like(*fg.shape)),
        in_specs=[VMEM] + [HBM] * 3 + [VMEM] * 2,
        out_specs=(VMEM,) * 7,
        scratch_shapes=[patch, patch, pltpu.SemaphoreType.DMA((5,))],
        compiler_params=params(16),
        cost_estimate=cost(44, 2_000_000),
        name="inner_taps",
    )(place, weights, mix_weight, fg, x_near, x_far)
    near_hidden, near_hg, near_rows = pl.pallas_call(
        functools.partial(near_kernel, columns),
        out_shape=(plane, plane, like(total_rows, channels, dtype=f32)),
        in_specs=[VMEM] * 8,
        out_specs=(VMEM,) * 3,
        scratch_shapes=[patch],
        compiler_params=params(16),
        cost_estimate=cost(38, 3_000_000),
        name="near_plane",
    )(place, x_near, x_far, x_pair, wide, fg_near, near_part, near_pulled)
    far_hidden, far_hg, grads = pl.pallas_call(
        functools.partial(far_kernel, columns, order),
        out_shape=(plane, plane, like(*grads_shape)),
        in_specs=[VMEM] * 10,
        out_specs=(VMEM,) * 3,
        scratch_shapes=[patch, pltpu.VMEM((total_rows, channels), f32)],
        compiler_params=params(16),
        cost_estimate=cost(38, 3_000_000),
        name="far_plane",
    )(place, x_near, x_far, x_cross, wide, fg_near, far_part, far_pulled, near_rows, near_hg)

    hg_cross = lax.ppermute(far_hg, "space", cross_swaps)
    if lots:
        size = devices // 4
        first = send(grads[2 * size : 3 * size], stages[0], 1)
        second = send(grads[3 * size :], stages[0], 1)
        hg_pair = second
    else:
        hg_pair = lax.ppermute(near_hg, "space", pair_swaps)
    features, input_grad = pl.pallas_call(
        functools.partial(backward_kernel, columns),
        out_shape=(like(planes, cells, width), like(planes, cells, channels)),
        in_specs=[VMEM] * 9,
        out_specs=(VMEM, VMEM),
        scratch_shapes=[patch, patch, pltpu.VMEM((cells, channels), bf16)],
        compiler_params=params(16),
        cost_estimate=cost(58, 2_000_000),
        name="features_and_input_grad",
    )(place, near_hg, far_hg, hg_pair, hg_cross, wide, mix_near, near_hidden, far_hidden)

    if lots:
        arrived = []
        for start, came, near in ((0, first, False), (size, second, True)):
            own, *others = pl.pallas_call(
                functools.partial(split_kernel, start),
                out_shape=[like(lot, piece, channels, dtype=f32)] + [like(lot, piece, channels)] * (chips - 1),
                in_specs=[VMEM, VMEM],
                out_specs=[VMEM] * chips,
                compiler_params=params(8),
                name="sum_of_core_pair",
            )(grads, came)
            came = [send(others[k - 1], stages[1], k) for k in (1, 3, 2)]
            parts = pl.pallas_call(
                functools.partial(gather_kernel, near),
                out_shape=[like(piece, channels, dtype=f32 if near and i == 0 else bf16) for i in range(lot)],
                in_specs=[pl.BlockSpec(memory_space=pl.ANY)] + [VMEM] * chips,
                out_specs=[VMEM] * lot,
                compiler_params=params(8),
                name="sum_of_chips",
            )(hg_cross, own, *came)
            for i in range(lot):
                k = i if near else lot + i
                arrived.append(send(parts[i], stages[2], k).astype(f32) if k else parts[i])
        total = sum(arrived[1:], arrived[0])
    else:
        flat = grads.reshape(-1)
        flat = jnp.pad(flat, (0, share * devices - flat.size))
        held = flat.reshape(dp_digits[::-1] + space_digits[::-1] + [share])
        places = {}
        for spot, stage in enumerate(stages_of("dp", dp_digits)[::-1] + stages_of("space", space_digits)[::-1]):
            places[stage] = spot
            mine = lax.rem(lax.axis_index(stage[0]) // stage[1], stage[2])
            held = jnp.take(held, apart(jnp.arange(stage[2]), mine, stage[2]), axis=spot)
        parts = jnp.transpose(held, [places[stage] for stage in stages] + [len(stages)])
        for stage in stages:
            total = parts[0].astype(f32)
            for term in [send(parts[k], stage, k) for k in range(1, stage[2])]:
                total = total + term.astype(f32)
            parts = total.astype(bf16)
    weight_grads = (total / devices).reshape(-1)
    return (features.reshape(feature_grad.shape), input_grad.reshape(universes.shape), weight_grads)


def solution(mesh):
    return jax.shard_map(
        shards,
        mesh=mesh,
        in_specs=(P("dp", "space", None, None, None), P(), P(), P("dp", "space", None, None, None)),
        out_specs=(
            P("dp", "space", None, None, None),
            P("dp", "space", None, None, None),
            P(("dp", "space")),
        ),
        check_vma=False,
    )
```

```python
import functools

import jax
import jax.numpy as jnp
from jax import lax
from jax.experimental import pallas as pl
from jax.experimental.pallas import tpu as pltpu
from jax.sharding import PartitionSpec as P

leak_slope = 0.3
bf16 = jnp.bfloat16
f32 = jnp.float32
NT = (((1,), (1,)), ((), ()))
TN = (((0,), (0,)), ((), ()))
VMEM = pl.BlockSpec(memory_space=pltpu.VMEM)
HBM = pl.BlockSpec(memory_space=pltpu.HBM)

FAR_ROUNDS = (((0, 2), (2, 1), (1, 3), (3, 0)), ((0, 3), (3, 1), (1, 2), (2, 0)))


def turn():
    parity = lax.rem(lax.axis_index("space"), 2)
    return parity, 2 * parity


def columns_kernel(columns, place_ref):
    place_ref[...] = lax.rem(lax.broadcasted_iota(jnp.int32, place_ref.shape, 0), columns)


def shift_columns(value, step, columns, place):
    moved = pltpu.roll(value, step % value.shape[0], 0)
    return jnp.where(place == (0 if step == 1 else columns - 1), 0.0, moved)


def join_columns(parts, step, columns, place):
    channels = parts.shape[1] // 3
    return (
        parts[:, channels : 2 * channels]
        + shift_columns(parts[:, :channels], step, columns, place)
        + shift_columns(parts[:, 2 * channels :], -step, columns, place)
    )


def spread_columns(hg, columns, place):
    value = hg.astype(f32)
    return jnp.concatenate(
        [
            shift_columns(value, -1, columns, place).astype(bf16),
            hg,
            shift_columns(value, 1, columns, place).astype(bf16),
        ],
        axis=1,
    )


def fill_rows(patch, a, plane, columns, mirror):
    cells, channels = plane.shape
    edge = jnp.zeros((columns, channels), plane.dtype)
    for b in range(3):
        at = a * 3 + b
        step = 1 - b if mirror else b - 1
        if step == 0:
            patch[at] = plane[...]
        elif step < 0:
            patch[at, pl.ds(0, columns), :] = edge
            patch[at, pl.ds(columns, cells - columns), :] = plane[pl.ds(0, cells - columns), :]
        else:
            patch[at, pl.ds(0, cells - columns), :] = plane[pl.ds(columns, cells - columns), :]
            patch[at, pl.ds(cells - columns, columns), :] = edge


def taps_dot(patch, wide, taps):
    return jnp.dot(
        jnp.concatenate([patch[t] for t in taps], axis=1),
        jnp.concatenate([wide[t] for t in taps], axis=0),
        preferred_element_type=f32,
    )


def clear_outside(patch, a):
    index = lax.axis_index("space")

    @pl.when(jnp.logical_or(index == 0, index == lax.axis_size("space") - 1))
    def _():
        for b in range(3):
            patch[a * 3 + b] = jnp.zeros(patch.shape[1:], patch.dtype)


def activate(summed, pulled, hidden_ref, hg_ref):
    hidden_ref[0] = jnp.where(summed > 0, summed, leak_slope * summed).astype(bf16)
    hg_ref[0] = (pulled * jnp.where(summed > 0, 1.0, leak_slope)).astype(bf16)


def kernel_grads(columns, place, patch, hidden_ref, hg_ref, fg, rows_ref, before_ref):
    channels = hidden_ref.shape[2]
    width = fg.shape[1]
    wide_hg = spread_columns(hg_ref[0], columns, place)
    for ab in range(9):
        block = lax.dot_general(patch[ab], wide_hg, TN, preferred_element_type=f32)
        for e in range(3):
            rows = pl.ds((ab * 3 + e) * channels, channels)
            value = block[:, e * channels : (e + 1) * channels]
            rows_ref[rows, :] = value if before_ref is None else value + before_ref[rows, :]
    mixed = lax.dot_general(hidden_ref[0], fg, TN, preferred_element_type=f32)
    parts = width // channels
    for j in range(parts):
        rows = pl.ds(27 * channels + j, channels, stride=parts)
        value = mixed[:, j * channels : (j + 1) * channels]
        rows_ref[rows, :] = value if before_ref is None else value + before_ref[rows, :]


def inner_kernel(columns, place_ref, w_hbm, mix_hbm, fg_hbm, near_ref, far_ref,
                 near_part, far_part, near_pulled, far_pulled, wide, mix_ref, fg_ref,
                 near_patch, far_patch, sems):
    channels = near_ref.shape[2]
    parity, side = turn()
    copies = [
        pltpu.make_async_copy(fg_hbm, fg_ref, sems.at[0]),
        pltpu.make_async_copy(mix_hbm, mix_ref, sems.at[1]),
    ]
    for e in range(3):
        copies.append(pltpu.make_async_copy(
            w_hbm.at[:, e], wide.at[:, :, pl.ds(e * channels, channels)], sems.at[2 + e]
        ))
    for copy in copies:
        copy.start()
    fill_rows(near_patch, 1, near_ref.at[0], columns, False)
    fill_rows(near_patch, side, far_ref.at[0], columns, False)
    fill_rows(far_patch, 1, far_ref.at[0], columns, False)
    fill_rows(far_patch, 2 - side, near_ref.at[0], columns, False)
    for copy in copies[:2]:
        copy.wait()
    near_pulled[...] = lax.dot_general(fg_ref[1 - parity], mix_ref[...], NT, preferred_element_type=f32)
    far_pulled[...] = lax.dot_general(fg_ref[parity], mix_ref[...], NT, preferred_element_type=f32)
    for copy in copies[2:]:
        copy.wait()
    for part, patch, a in ((near_part, near_patch, side), (far_part, far_patch, 2 - side)):
        taps = [3, 4, 5] + [a * 3 + b for b in range(3)]
        part[...] = join_columns(taps_dot(patch, wide, taps), 1, columns, place_ref[...])


def finish_plane(columns, place, patch, a, wide, part_ref, pulled_ref, fg, before_ref, hidden_ref, hg_ref, rows_ref):
    taps = [a * 3 + b for b in range(3)]
    summed = part_ref[...] + join_columns(taps_dot(patch, wide, taps), 1, columns, place)
    activate(summed, pulled_ref[...], hidden_ref, hg_ref)
    kernel_grads(columns, place, patch, hidden_ref, hg_ref, fg, rows_ref, before_ref)


def near_kernel(columns, place_ref, near_ref, far_ref, pair_ref, wide, fg_ref, part_ref, pulled_ref,
                hidden_ref, hg_ref, rows_ref, patch):
    parity, side = turn()
    fill_rows(patch, 2 - side, pair_ref.at[0], columns, False)
    fill_rows(patch, 1, near_ref.at[0], columns, False)
    fill_rows(patch, side, far_ref.at[0], columns, False)
    finish_plane(columns, place_ref[...], patch, 2 - side, wide, part_ref, pulled_ref, fg_ref[1 - parity], None,
                 hidden_ref, hg_ref, rows_ref)


def far_kernel(columns, order, place_ref, near_ref, far_ref, cross_ref, wide, fg_ref, part_ref, pulled_ref, before_ref,
               near_hg,
               hidden_ref, hg_ref, grads_ref, patch, rows_ref):
    parity, side = turn()
    fill_rows(patch, side, cross_ref.at[0], columns, False)
    clear_outside(patch, side)
    fill_rows(patch, 1, far_ref.at[0], columns, False)
    fill_rows(patch, 2 - side, near_ref.at[0], columns, False)
    finish_plane(columns, place_ref[...], patch, side, wide, part_ref, pulled_ref, fg_ref[parity], before_ref,
                 hidden_ref, hg_ref, rows_ref)
    if order is None:
        grads_ref[...] = rows_ref[...].astype(bf16)
    else:
        piece = grads_ref.shape[1]
        spots = order()
        for k, spot in enumerate(spots):
            grads_ref[spot] = rows_ref[pl.ds(k * piece, piece), :].astype(bf16)
        for spot, first, rows in runs_of(near_hg.shape[1], piece):
            grads_ref[len(spots) + spot, pl.ds(0, rows), :] = near_hg[0, pl.ds(first, rows), :]


def runs_of(cells, piece):
    step = piece // 16 * 16
    return [(spot, first, min(step, cells - first)) for spot, first in enumerate(range(0, cells, step))]


def split_kernel(start, kept_ref, came_ref, own_ref, *out_refs):
    lot = own_ref.shape[0]
    for chip in range(len(out_refs) + 1):
        for i in range(lot):
            at = chip * lot + i
            value = kept_ref[start + at].astype(f32) + came_ref[at].astype(f32)
            if chip == 0:
                own_ref[i] = value
            else:
                out_refs[chip - 1][i] = value.astype(bf16)


def gather_kernel(keeps, after_ref, own_ref, *refs):
    lot = own_ref.shape[0]
    came, out = refs[: len(refs) - lot], refs[len(refs) - lot :]
    for i in range(lot):
        value = own_ref[i]
        for ref in came:
            value = value + ref[i].astype(f32)
        out[i][...] = value if keeps and i == 0 else value.astype(bf16)


def backward_kernel(columns, place_ref, near_ref, far_ref, pair_ref, cross_ref, wide, mix_ref, near_hidden, far_hidden,
                    features_ref, input_ref, near_patch, far_patch, pair_plane):
    cells, channels = near_ref.shape[1:]
    if pair_ref.shape[1] == cells:
        pair_plane[...] = pair_ref[0]
    else:
        spots = runs_of(cells, pair_ref.shape[1])
        start = pair_ref.shape[0] - len(spots)
        for spot, first, rows in spots:
            pair_plane[pl.ds(first, rows), :] = pair_ref[start + spot, pl.ds(0, rows), :]
    parity, side = turn()
    features_ref[1 - parity] = jnp.dot(near_hidden[0], mix_ref[...], preferred_element_type=f32).astype(bf16)
    features_ref[parity] = jnp.dot(far_hidden[0], mix_ref[...], preferred_element_type=f32).astype(bf16)
    fill_rows(near_patch, side, pair_plane, columns, True)
    fill_rows(near_patch, 1, near_ref.at[0], columns, True)
    fill_rows(near_patch, 2 - side, far_ref.at[0], columns, True)
    fill_rows(far_patch, side, near_ref.at[0], columns, True)
    fill_rows(far_patch, 1, far_ref.at[0], columns, True)
    fill_rows(far_patch, 2 - side, cross_ref.at[0], columns, True)
    clear_outside(far_patch, 2 - side)
    for patch, plane in ((near_patch, 1 - parity), (far_patch, parity)):
        parts = jnp.zeros((near_ref.shape[1], 3 * channels), f32)
        for first in range(0, 9, 2):
            taps = range(first, min(first + 2, 9))
            block = jnp.concatenate(
                [
                    jnp.concatenate([wide[t, :, e * channels : (e + 1) * channels] for e in range(3)], axis=0)
                    for t in taps
                ],
                axis=1,
            )
            parts = parts + lax.dot_general(
                jnp.concatenate([patch[t] for t in taps], axis=1), block, NT, preferred_element_type=f32
            )
        input_ref[plane] = join_columns(parts, -1, columns, place_ref[...]).astype(bf16)


def digits_of(count):
    digits = []
    while count > 1:
        for radix in (2, 3, 5, 7, count) if not digits else (4, 2, 3, 5, 7, count):
            if count % radix == 0:
                digits.append(radix)
                count //= radix
                break
    return digits


def stages_of(axis, digits):
    stages, stride = [], 1
    for radix in digits:
        stages.append((axis, stride, radix))
        stride *= radix
    return stages


def apart(digit, mine, radix):
    if radix & (radix - 1) == 0:
        return lax.bitwise_xor(mine, digit)
    return lax.rem(digit - mine + radix, radix)


def send(value, stage, k):
    axis, stride, radix = stage
    pairs = []
    for i in range(lax.axis_size(axis)):
        digit = i // stride % radix
        other = digit ^ k if radix & (radix - 1) == 0 else (digit + k) % radix
        pairs.append((i, i + (other - digit) * stride))
    return lax.ppermute(value, axis, pairs)


def swaps(start, count):
    found = []
    for i in range(start, count + start, 2):
        found += [(i, (i + 1) % count), ((i + 1) % count, i)]
    return found


def shards(universes, conv_weight, mix_weight, feature_grad):
    channels = conv_weight.shape[1]
    width = mix_weight.shape[1]
    planes, map_rows, columns = universes.shape[1:4]
    if planes != 2 or lax.axis_size("space") % 2:
        raise ValueError("slab shape")
    cells = map_rows * columns
    group_count, slab_count = lax.axis_size("dp"), lax.axis_size("space")
    devices = group_count * slab_count
    space_digits = digits_of(slab_count)
    dp_digits = [4] if group_count == 4 else digits_of(group_count)
    stages = stages_of("space", space_digits) + stages_of("dp", dp_digits)

    x = universes.reshape(planes, cells, channels)
    fg = feature_grad.reshape(planes, cells, width)
    weights = conv_weight.reshape(9, 3, channels, channels)
    pair_swaps, cross_swaps = swaps(0, slab_count), swaps(1, slab_count)

    parity = lax.rem(lax.axis_index("space"), 2)
    x_near = lax.dynamic_slice_in_dim(x, 1 - parity, 1, 0)
    x_far = lax.dynamic_slice_in_dim(x, parity, 1, 0)
    x_cross = lax.ppermute(x_far, "space", cross_swaps)
    x_pair = lax.ppermute(x_near, "space", pair_swaps)

    total_rows = 27 * channels + channels * width // channels
    share = (total_rows * channels + devices - 1) // devices
    lots = (
        share * devices == total_rows * channels
        and share % channels == 0
        and len(stages) == 3
        and stages[0][2] == 2
        and stages[2][2] == 4
    )
    if lots:
        piece = share // channels
        chips, groups = stages[1][2], stages[2][2]
        lot = groups // 2
        grads_shape = (devices + len(runs_of(cells, piece)), piece, channels)

        def order():
            def relative(stage):
                axis, stride, radix = stage
                mine = lax.rem(lax.div(lax.axis_index(axis), stride), radix)
                return [apart(digit, mine, radix) for digit in range(radix)]

            cores = [core * (2 * chips * lot) for core in relative(stages[0])]
            chip_spots = [chip * lot for chip in relative(stages[1])]
            mine = lax.axis_index("dp")
            late = lax.div(mine, lot)
            group_spots = []
            for group in relative(stages[2]):
                near = 1 - lax.div(group, lot)
                group_spots.append(near * (chips * lot) + lax.rem(group + (1 - near) * late, lot))
            spots = []
            for k in range(devices):
                group, place = divmod(k, slab_count)
                chip, core = divmod(place, 2)
                spots.append(cores[core] + chip_spots[chip] + group_spots[group])
            return spots
    else:
        grads_shape = (total_rows, channels)
        order = None

    def like(*shape, dtype=bf16):
        return jax.ShapeDtypeStruct(shape, dtype)

    def params(mebibytes):
        return pltpu.CompilerParams(vmem_limit_bytes=mebibytes * 1024 * 1024)

    def cost(blocks, read):
        return pl.CostEstimate(
            flops=2 * cells * channels * channels * blocks, bytes_accessed=read, transcendentals=0
        )

    plane = like(1, cells, channels)
    plane_sum = like(cells, channels, dtype=f32)
    patch = pltpu.VMEM((9, cells, channels), bf16)
    place = pl.pallas_call(
        functools.partial(columns_kernel, columns),
        out_shape=like(cells, channels, dtype=jnp.int32),
        out_specs=VMEM,
        compiler_params=params(4),
        cost_estimate=cost(100, 8_000_000),
        name="columns_of_cells",
    )()
    near_part, far_part, near_pulled, far_pulled, wide, mix_near, fg_near = pl.pallas_call(
        functools.partial(inner_kernel, columns),
        out_shape=(plane_sum,) * 4
        + (like(9, channels, 3 * channels), like(*mix_weight.shape), like(*fg.shape)),
        in_specs=[VMEM] + [HBM] * 3 + [VMEM] * 2,
        out_specs=(VMEM,) * 7,
        scratch_shapes=[patch, patch, pltpu.SemaphoreType.DMA((5,))],
        compiler_params=params(16),
        cost_estimate=cost(44, 2_000_000),
        name="inner_taps",
    )(place, weights, mix_weight, fg, x_near, x_far)
    near_hidden, near_hg, near_rows = pl.pallas_call(
        functools.partial(near_kernel, columns),
        out_shape=(plane, plane, like(total_rows, channels, dtype=f32)),
        in_specs=[VMEM] * 8,
        out_specs=(VMEM,) * 3,
        scratch_shapes=[patch],
        compiler_params=params(16),
        cost_estimate=cost(38, 3_000_000),
        name="near_plane",
    )(place, x_near, x_far, x_pair, wide, fg_near, near_part, near_pulled)
    far_hidden, far_hg, grads = pl.pallas_call(
        functools.partial(far_kernel, columns, order),
        out_shape=(plane, plane, like(*grads_shape)),
        in_specs=[VMEM] * 10,
        out_specs=(VMEM,) * 3,
        scratch_shapes=[patch, pltpu.VMEM((total_rows, channels), f32)],
        compiler_params=params(16),
        cost_estimate=cost(38, 3_000_000),
        name="far_plane",
    )(place, x_near, x_far, x_cross, wide, fg_near, far_part, far_pulled, near_rows, near_hg)

    hg_cross = lax.ppermute(far_hg, "space", cross_swaps)
    if lots:
        size = devices // 4
        first = send(grads[2 * size : 3 * size], stages[0], 1)
        second = send(grads[3 * size :], stages[0], 1)
        hg_pair = second
    else:
        hg_pair = lax.ppermute(near_hg, "space", pair_swaps)
    features, input_grad = pl.pallas_call(
        functools.partial(backward_kernel, columns),
        out_shape=(like(planes, cells, width), like(planes, cells, channels)),
        in_specs=[VMEM] * 9,
        out_specs=(VMEM, VMEM),
        scratch_shapes=[patch, patch, pltpu.VMEM((cells, channels), bf16)],
        compiler_params=params(16),
        cost_estimate=cost(58, 2_000_000),
        name="features_and_input_grad",
    )(place, near_hg, far_hg, hg_pair, hg_cross, wide, mix_near, near_hidden, far_hidden)

    if lots:
        arrived = []
        for start, came, near in ((0, first, False), (size, second, True)):
            own, *others = pl.pallas_call(
                functools.partial(split_kernel, start),
                out_shape=[like(lot, piece, channels, dtype=f32)] + [like(lot, piece, channels)] * (chips - 1),
                in_specs=[VMEM, VMEM],
                out_specs=[VMEM] * chips,
                compiler_params=params(8),
                name="sum_of_core_pair",
            )(grads, came)
            came = [send(others[k - 1], stages[1], k) for k in (1, 3, 2)]
            parts = pl.pallas_call(
                functools.partial(gather_kernel, near),
                out_shape=[like(piece, channels, dtype=f32 if near and i == 0 else bf16) for i in range(lot)],
                in_specs=[pl.BlockSpec(memory_space=pl.ANY)] + [VMEM] * chips,
                out_specs=[VMEM] * lot,
                compiler_params=params(8),
                name="sum_of_chips",
            )(hg_cross, own, *came)
            if near:
                arrived += [parts[0], send(parts[1], stages[2], 1).astype(f32)]
            else:
                arrived += [lax.ppermute(part, "dp", pairs).astype(f32) for part, pairs in zip(parts, FAR_ROUNDS)]
        total = sum(arrived[1:], arrived[0])
    else:
        flat = grads.reshape(-1)
        flat = jnp.pad(flat, (0, share * devices - flat.size))
        held = flat.reshape(dp_digits[::-1] + space_digits[::-1] + [share])
        places = {}
        for spot, stage in enumerate(stages_of("dp", dp_digits)[::-1] + stages_of("space", space_digits)[::-1]):
            places[stage] = spot
            mine = lax.rem(lax.axis_index(stage[0]) // stage[1], stage[2])
            held = jnp.take(held, apart(jnp.arange(stage[2]), mine, stage[2]), axis=spot)
        parts = jnp.transpose(held, [places[stage] for stage in stages] + [len(stages)])
        for stage in stages:
            total = parts[0].astype(f32)
            for term in [send(parts[k], stage, k) for k in range(1, stage[2])]:
                total = total + term.astype(f32)
            parts = total.astype(bf16)
    weight_grads = (total / devices).reshape(-1)
    return (features.reshape(feature_grad.shape), input_grad.reshape(universes.shape), weight_grads)


def solution(mesh):
    return jax.shard_map(
        shards,
        mesh=mesh,
        in_specs=(P("dp", "space", None, None, None), P(), P(), P("dp", "space", None, None, None)),
        out_specs=(
            P("dp", "space", None, None, None),
            P("dp", "space", None, None, None),
            P(("dp", "space")),
        ),
        check_vma=False,
    )
```

```python
import functools

import jax
import jax.numpy as jnp
from jax import lax
from jax.experimental import pallas as pl
from jax.experimental.pallas import tpu as pltpu
from jax.sharding import PartitionSpec as P

leak_slope = 0.3
bf16 = jnp.bfloat16
f32 = jnp.float32
NT = (((1,), (1,)), ((), ()))
TN = (((0,), (0,)), ((), ()))
VMEM = pl.BlockSpec(memory_space=pltpu.VMEM)
HBM = pl.BlockSpec(memory_space=pltpu.HBM)

FAR_ROUNDS = (((0, 2), (2, 1), (1, 3), (3, 0)), ((0, 3), (3, 1), (1, 2), (2, 0)))


def turn():
    parity = lax.rem(lax.axis_index("space"), 2)
    return parity, 2 * parity


def columns_kernel(columns, place_ref):
    place_ref[...] = lax.rem(lax.broadcasted_iota(jnp.int32, place_ref.shape, 0), columns)


def shift_columns(value, step, columns, place):
    moved = pltpu.roll(value, step % value.shape[0], 0)
    return jnp.where(place == (0 if step == 1 else columns - 1), 0.0, moved)


def join_columns(parts, step, columns, place):
    channels = parts.shape[1] // 3
    return (
        parts[:, channels : 2 * channels]
        + shift_columns(parts[:, :channels], step, columns, place)
        + shift_columns(parts[:, 2 * channels :], -step, columns, place)
    )


def spread_columns(hg, columns, place):
    value = hg.astype(f32)
    return jnp.concatenate(
        [
            shift_columns(value, -1, columns, place).astype(bf16),
            hg,
            shift_columns(value, 1, columns, place).astype(bf16),
        ],
        axis=1,
    )


def fill_rows(patch, a, plane, columns, mirror):
    cells, channels = plane.shape
    edge = jnp.zeros((columns, channels), plane.dtype)
    for b in range(3):
        at = a * 3 + b
        step = 1 - b if mirror else b - 1
        if step == 0:
            patch[at] = plane[...]
        elif step < 0:
            patch[at, pl.ds(0, columns), :] = edge
            patch[at, pl.ds(columns, cells - columns), :] = plane[pl.ds(0, cells - columns), :]
        else:
            patch[at, pl.ds(0, cells - columns), :] = plane[pl.ds(columns, cells - columns), :]
            patch[at, pl.ds(cells - columns, columns), :] = edge


def taps_dot(patch, wide, taps):
    return jnp.dot(
        jnp.concatenate([patch[t] for t in taps], axis=1),
        jnp.concatenate([wide[t] for t in taps], axis=0),
        preferred_element_type=f32,
    )


def clear_outside(patch, a):
    index = lax.axis_index("space")

    @pl.when(jnp.logical_or(index == 0, index == lax.axis_size("space") - 1))
    def _():
        for b in range(3):
            patch[a * 3 + b] = jnp.zeros(patch.shape[1:], patch.dtype)


def activate(summed, pulled, hidden_ref, hg_ref):
    hidden_ref[0] = jnp.where(summed > 0, summed, leak_slope * summed).astype(bf16)
    hg_ref[0] = (pulled * jnp.where(summed > 0, 1.0, leak_slope)).astype(bf16)


def kernel_grads(columns, place, patch, hidden_ref, hg_ref, fg, rows_ref, before_ref):
    channels = hidden_ref.shape[2]
    width = fg.shape[1]
    wide_hg = spread_columns(hg_ref[0], columns, place)
    for ab in range(9):
        block = lax.dot_general(patch[ab], wide_hg, TN, preferred_element_type=f32)
        for e in range(3):
            rows = pl.ds((ab * 3 + e) * channels, channels)
            value = block[:, e * channels : (e + 1) * channels]
            rows_ref[rows, :] = value if before_ref is None else value + before_ref[rows, :]
    mixed = lax.dot_general(hidden_ref[0], fg, TN, preferred_element_type=f32)
    parts = width // channels
    for j in range(parts):
        rows = pl.ds(27 * channels + j, channels, stride=parts)
        value = mixed[:, j * channels : (j + 1) * channels]
        rows_ref[rows, :] = value if before_ref is None else value + before_ref[rows, :]


def inner_kernel(columns, place_ref, w_hbm, mix_hbm, fg_hbm, near_ref, far_ref,
                 near_part, far_part, near_pulled, far_pulled, wide, mix_ref, fg_ref,
                 near_patch, far_patch, sems):
    channels = near_ref.shape[2]
    parity, side = turn()
    copies = [
        pltpu.make_async_copy(fg_hbm, fg_ref, sems.at[0]),
        pltpu.make_async_copy(mix_hbm, mix_ref, sems.at[1]),
    ]
    for e in range(3):
        copies.append(pltpu.make_async_copy(
            w_hbm.at[:, e], wide.at[:, :, pl.ds(e * channels, channels)], sems.at[2 + e]
        ))
    for copy in copies:
        copy.start()
    fill_rows(near_patch, 1, near_ref.at[0], columns, False)
    fill_rows(near_patch, side, far_ref.at[0], columns, False)
    fill_rows(far_patch, 1, far_ref.at[0], columns, False)
    fill_rows(far_patch, 2 - side, near_ref.at[0], columns, False)
    for copy in copies[:2]:
        copy.wait()
    near_pulled[...] = lax.dot_general(fg_ref[1 - parity], mix_ref[...], NT, preferred_element_type=f32)
    far_pulled[...] = lax.dot_general(fg_ref[parity], mix_ref[...], NT, preferred_element_type=f32)
    for copy in copies[2:]:
        copy.wait()
    for part, patch, a in ((near_part, near_patch, side), (far_part, far_patch, 2 - side)):
        taps = [3, 4, 5] + [a * 3 + b for b in range(3)]
        part[...] = join_columns(taps_dot(patch, wide, taps), 1, columns, place_ref[...])


def finish_plane(columns, place, patch, a, wide, part_ref, pulled_ref, fg, before_ref, hidden_ref, hg_ref, rows_ref):
    taps = [a * 3 + b for b in range(3)]
    summed = part_ref[...] + join_columns(taps_dot(patch, wide, taps), 1, columns, place)
    activate(summed, pulled_ref[...], hidden_ref, hg_ref)
    kernel_grads(columns, place, patch, hidden_ref, hg_ref, fg, rows_ref, before_ref)


def near_kernel(columns, place_ref, near_ref, far_ref, pair_ref, wide, fg_ref, part_ref, pulled_ref,
                hidden_ref, hg_ref, rows_ref, patch):
    parity, side = turn()
    fill_rows(patch, 2 - side, pair_ref.at[0], columns, False)
    fill_rows(patch, 1, near_ref.at[0], columns, False)
    fill_rows(patch, side, far_ref.at[0], columns, False)
    finish_plane(columns, place_ref[...], patch, 2 - side, wide, part_ref, pulled_ref, fg_ref[1 - parity], None,
                 hidden_ref, hg_ref, rows_ref)


def far_kernel(columns, order, place_ref, near_ref, far_ref, cross_ref, wide, fg_ref, part_ref, pulled_ref, before_ref,
               near_hg,
               hidden_ref, hg_ref, grads_ref, patch, rows_ref):
    parity, side = turn()
    fill_rows(patch, side, cross_ref.at[0], columns, False)
    clear_outside(patch, side)
    fill_rows(patch, 1, far_ref.at[0], columns, False)
    fill_rows(patch, 2 - side, near_ref.at[0], columns, False)
    finish_plane(columns, place_ref[...], patch, side, wide, part_ref, pulled_ref, fg_ref[parity], before_ref,
                 hidden_ref, hg_ref, rows_ref)
    if order is None:
        grads_ref[...] = rows_ref[...].astype(bf16)
    else:
        piece = grads_ref.shape[1]
        spots = order()
        for k, spot in enumerate(spots):
            grads_ref[spot] = rows_ref[pl.ds(k * piece, piece), :].astype(bf16)
        for spot, first, rows in runs_of(near_hg.shape[1], piece):
            grads_ref[len(spots) + spot, pl.ds(0, rows), :] = near_hg[0, pl.ds(first, rows), :]


def runs_of(cells, piece):
    step = piece // 16 * 16
    return [(spot, first, min(step, cells - first)) for spot, first in enumerate(range(0, cells, step))]


def split_kernel(start, kept_ref, came_ref, own_ref, *out_refs):
    lot = own_ref.shape[0]
    for chip in range(len(out_refs) + 1):
        for i in range(lot):
            at = chip * lot + i
            value = kept_ref[start + at].astype(f32) + came_ref[at].astype(f32)
            if chip == 0:
                own_ref[i] = value
            else:
                out_refs[chip - 1][i] = value.astype(bf16)


def gather_kernel(keeps, after_ref, own_ref, *refs):
    lot = own_ref.shape[0]
    came, out = refs[: len(refs) - lot], refs[len(refs) - lot :]
    for i in range(lot):
        value = own_ref[i]
        for ref in came:
            value = value + ref[i].astype(f32)
        out[i][...] = value if keeps and i == 0 else value.astype(bf16)


def backward_kernel(columns, place_ref, near_ref, far_ref, pair_ref, cross_ref, wide, mix_ref, near_hidden, far_hidden,
                    features_ref, input_ref, near_patch, far_patch, pair_plane):
    cells, channels = near_ref.shape[1:]
    if pair_ref.shape[1] == cells:
        pair_plane[...] = pair_ref[0]
    else:
        spots = runs_of(cells, pair_ref.shape[1])
        start = pair_ref.shape[0] - len(spots)
        for spot, first, rows in spots:
            pair_plane[pl.ds(first, rows), :] = pair_ref[start + spot, pl.ds(0, rows), :]
    parity, side = turn()
    features_ref[1 - parity] = jnp.dot(near_hidden[0], mix_ref[...], preferred_element_type=f32).astype(bf16)
    features_ref[parity] = jnp.dot(far_hidden[0], mix_ref[...], preferred_element_type=f32).astype(bf16)
    fill_rows(near_patch, side, pair_plane, columns, True)
    fill_rows(near_patch, 1, near_ref.at[0], columns, True)
    fill_rows(near_patch, 2 - side, far_ref.at[0], columns, True)
    fill_rows(far_patch, side, near_ref.at[0], columns, True)
    fill_rows(far_patch, 1, far_ref.at[0], columns, True)
    fill_rows(far_patch, 2 - side, cross_ref.at[0], columns, True)
    clear_outside(far_patch, 2 - side)
    for patch, plane in ((near_patch, 1 - parity), (far_patch, parity)):
        parts = jnp.zeros((near_ref.shape[1], 3 * channels), f32)
        for first in range(0, 9, 2):
            taps = range(first, min(first + 2, 9))
            block = jnp.concatenate(
                [
                    jnp.concatenate([wide[t, :, e * channels : (e + 1) * channels] for e in range(3)], axis=0)
                    for t in taps
                ],
                axis=1,
            )
            parts = parts + lax.dot_general(
                jnp.concatenate([patch[t] for t in taps], axis=1), block, NT, preferred_element_type=f32
            )
        input_ref[plane] = join_columns(parts, -1, columns, place_ref[...]).astype(bf16)


def digits_of(count):
    digits = []
    while count > 1:
        for radix in (2, 3, 5, 7, count) if not digits else (4, 2, 3, 5, 7, count):
            if count % radix == 0:
                digits.append(radix)
                count //= radix
                break
    return digits


def stages_of(axis, digits):
    stages, stride = [], 1
    for radix in digits:
        stages.append((axis, stride, radix))
        stride *= radix
    return stages


def apart(digit, mine, radix):
    if radix & (radix - 1) == 0:
        return lax.bitwise_xor(mine, digit)
    return lax.rem(digit - mine + radix, radix)


def send(value, stage, k):
    axis, stride, radix = stage
    pairs = []
    for i in range(lax.axis_size(axis)):
        digit = i // stride % radix
        other = digit ^ k if radix & (radix - 1) == 0 else (digit + k) % radix
        pairs.append((i, i + (other - digit) * stride))
    return lax.ppermute(value, axis, pairs)


def swaps(start, count):
    found = []
    for i in range(start, count + start, 2):
        found += [(i, (i + 1) % count), ((i + 1) % count, i)]
    return found


def shards(universes, conv_weight, mix_weight, feature_grad):
    channels = conv_weight.shape[1]
    width = mix_weight.shape[1]
    planes, map_rows, columns = universes.shape[1:4]
    if planes != 2 or lax.axis_size("space") % 2:
        raise ValueError("slab shape")
    cells = map_rows * columns
    group_count, slab_count = lax.axis_size("dp"), lax.axis_size("space")
    devices = group_count * slab_count
    space_digits = digits_of(slab_count)
    dp_digits = [4] if group_count == 4 else digits_of(group_count)
    stages = stages_of("space", space_digits) + stages_of("dp", dp_digits)

    x = universes.reshape(planes, cells, channels)
    fg = feature_grad.reshape(planes, cells, width)
    weights = conv_weight.reshape(9, 3, channels, channels)
    pair_swaps, cross_swaps = swaps(0, slab_count), swaps(1, slab_count)

    parity = lax.rem(lax.axis_index("space"), 2)
    both = x.at[lax.bitwise_xor(1 - lax.iota(jnp.int32, 2), parity)].get(mode="promise_in_bounds")
    x_near, x_far = both[:1], both[1:]
    x_cross = lax.ppermute(x_far, "space", cross_swaps)
    x_pair = lax.ppermute(x_near, "space", pair_swaps)

    total_rows = 27 * channels + channels * width // channels
    share = (total_rows * channels + devices - 1) // devices
    lots = (
        share * devices == total_rows * channels
        and share % channels == 0
        and len(stages) == 3
        and stages[0][2] == 2
        and stages[2][2] == 4
    )
    if lots:
        piece = share // channels
        chips, groups = stages[1][2], stages[2][2]
        lot = groups // 2
        grads_shape = (devices + len(runs_of(cells, piece)), piece, channels)

        def order():
            def relative(stage):
                axis, stride, radix = stage
                mine = lax.rem(lax.div(lax.axis_index(axis), stride), radix)
                return [apart(digit, mine, radix) for digit in range(radix)]

            cores = [core * (2 * chips * lot) for core in relative(stages[0])]
            chip_spots = [chip * lot for chip in relative(stages[1])]
            mine = lax.axis_index("dp")
            late = lax.div(mine, lot)
            group_spots = []
            for group in relative(stages[2]):
                near = 1 - lax.div(group, lot)
                group_spots.append(near * (chips * lot) + lax.rem(group + (1 - near) * late, lot))
            spots = []
            for k in range(devices):
                group, place = divmod(k, slab_count)
                chip, core = divmod(place, 2)
                spots.append(cores[core] + chip_spots[chip] + group_spots[group])
            return spots
    else:
        grads_shape = (total_rows, channels)
        order = None

    def like(*shape, dtype=bf16):
        return jax.ShapeDtypeStruct(shape, dtype)

    def params(mebibytes):
        return pltpu.CompilerParams(vmem_limit_bytes=mebibytes * 1024 * 1024)

    def cost(blocks, read):
        return pl.CostEstimate(
            flops=2 * cells * channels * channels * blocks, bytes_accessed=read, transcendentals=0
        )

    plane = like(1, cells, channels)
    plane_sum = like(cells, channels, dtype=f32)
    patch = pltpu.VMEM((9, cells, channels), bf16)
    place = pl.pallas_call(
        functools.partial(columns_kernel, columns),
        out_shape=like(cells, channels, dtype=jnp.int32),
        out_specs=VMEM,
        compiler_params=params(4),
        cost_estimate=cost(100, 8_000_000),
        name="columns_of_cells",
    )()
    near_part, far_part, near_pulled, far_pulled, wide, mix_near, fg_near = pl.pallas_call(
        functools.partial(inner_kernel, columns),
        out_shape=(plane_sum,) * 4
        + (like(9, channels, 3 * channels), like(*mix_weight.shape), like(*fg.shape)),
        in_specs=[VMEM] + [HBM] * 3 + [VMEM] * 2,
        out_specs=(VMEM,) * 7,
        scratch_shapes=[patch, patch, pltpu.SemaphoreType.DMA((5,))],
        compiler_params=params(16),
        cost_estimate=cost(44, 2_000_000),
        name="inner_taps",
    )(place, weights, mix_weight, fg, x_near, x_far)
    near_hidden, near_hg, near_rows = pl.pallas_call(
        functools.partial(near_kernel, columns),
        out_shape=(plane, plane, like(total_rows, channels, dtype=f32)),
        in_specs=[VMEM] * 8,
        out_specs=(VMEM,) * 3,
        scratch_shapes=[patch],
        compiler_params=params(16),
        cost_estimate=cost(38, 3_000_000),
        name="near_plane",
    )(place, x_near, x_far, x_pair, wide, fg_near, near_part, near_pulled)
    far_hidden, far_hg, grads = pl.pallas_call(
        functools.partial(far_kernel, columns, order),
        out_shape=(plane, plane, like(*grads_shape)),
        in_specs=[VMEM] * 10,
        out_specs=(VMEM,) * 3,
        scratch_shapes=[patch, pltpu.VMEM((total_rows, channels), f32)],
        compiler_params=params(16),
        cost_estimate=cost(38, 3_000_000),
        name="far_plane",
    )(place, x_near, x_far, x_cross, wide, fg_near, far_part, far_pulled, near_rows, near_hg)

    hg_cross = lax.ppermute(far_hg, "space", cross_swaps)
    if lots:
        size = devices // 4
        first = send(grads[2 * size : 3 * size], stages[0], 1)
        second = send(grads[3 * size :], stages[0], 1)
        hg_pair = second
    else:
        hg_pair = lax.ppermute(near_hg, "space", pair_swaps)
    features, input_grad = pl.pallas_call(
        functools.partial(backward_kernel, columns),
        out_shape=(like(planes, cells, width), like(planes, cells, channels)),
        in_specs=[VMEM] * 9,
        out_specs=(VMEM, VMEM),
        scratch_shapes=[patch, patch, pltpu.VMEM((cells, channels), bf16)],
        compiler_params=params(16),
        cost_estimate=cost(58, 2_000_000),
        name="features_and_input_grad",
    )(place, near_hg, far_hg, hg_pair, hg_cross, wide, mix_near, near_hidden, far_hidden)

    if lots:
        arrived = []
        for start, came, near in ((0, first, False), (size, second, True)):
            own, *others = pl.pallas_call(
                functools.partial(split_kernel, start),
                out_shape=[like(lot, piece, channels, dtype=f32)] + [like(lot, piece, channels)] * (chips - 1),
                in_specs=[VMEM, VMEM],
                out_specs=[VMEM] * chips,
                compiler_params=params(8),
                name="sum_of_core_pair",
            )(grads, came)
            came = [send(others[k - 1], stages[1], k) for k in (1, 3, 2)]
            parts = pl.pallas_call(
                functools.partial(gather_kernel, near),
                out_shape=[like(piece, channels, dtype=f32 if near and i == 0 else bf16) for i in range(lot)],
                in_specs=[pl.BlockSpec(memory_space=pl.ANY)] + [VMEM] * chips,
                out_specs=[VMEM] * lot,
                compiler_params=params(8),
                name="sum_of_chips",
            )(hg_cross, own, *came)
            if near:
                arrived += [parts[0], send(parts[1], stages[2], 1).astype(f32)]
            else:
                arrived += [lax.ppermute(part, "dp", pairs).astype(f32) for part, pairs in zip(parts, FAR_ROUNDS)]
        total = sum(arrived[1:], arrived[0])
    else:
        flat = grads.reshape(-1)
        flat = jnp.pad(flat, (0, share * devices - flat.size))
        held = flat.reshape(dp_digits[::-1] + space_digits[::-1] + [share])
        places = {}
        for spot, stage in enumerate(stages_of("dp", dp_digits)[::-1] + stages_of("space", space_digits)[::-1]):
            places[stage] = spot
            mine = lax.rem(lax.axis_index(stage[0]) // stage[1], stage[2])
            held = jnp.take(held, apart(jnp.arange(stage[2]), mine, stage[2]), axis=spot)
        parts = jnp.transpose(held, [places[stage] for stage in stages] + [len(stages)])
        for stage in stages:
            total = parts[0].astype(f32)
            for term in [send(parts[k], stage, k) for k in range(1, stage[2])]:
                total = total + term.astype(f32)
            parts = total.astype(bf16)
    weight_grads = (total / devices).reshape(-1)
    return (features.reshape(feature_grad.shape), input_grad.reshape(universes.shape), weight_grads)


def solution(mesh):
    return jax.shard_map(
        shards,
        mesh=mesh,
        in_specs=(P("dp", "space", None, None, None), P(), P(), P("dp", "space", None, None, None)),
        out_specs=(
            P("dp", "space", None, None, None),
            P("dp", "space", None, None, None),
            P(("dp", "space")),
        ),
        check_vma=False,
    )
```

```python
import functools

import jax
import jax.numpy as jnp
from jax import lax
from jax.experimental import pallas as pl
from jax.experimental.pallas import tpu as pltpu
from jax.sharding import PartitionSpec as P

leak_slope = 0.3
bf16 = jnp.bfloat16
f32 = jnp.float32
NT = (((1,), (1,)), ((), ()))
TN = (((0,), (0,)), ((), ()))
VMEM = pl.BlockSpec(memory_space=pltpu.VMEM)
HBM = pl.BlockSpec(memory_space=pltpu.HBM)

CHIP_ROUNDS = (
    ((0, 1), (1, 3), (3, 2), (2, 0)),
    ((0, 2), (2, 3), (3, 1), (1, 0)),
    ((0, 3), (3, 0), (1, 2), (2, 1)),
)
FAR_ROUNDS = (((0, 2), (2, 1), (1, 3), (3, 0)), ((0, 3), (3, 1), (1, 2), (2, 0)))


def turn():
    parity = lax.rem(lax.axis_index("space"), 2)
    return parity, 2 * parity


def columns_kernel(columns, place_ref):
    place_ref[...] = lax.rem(lax.broadcasted_iota(jnp.int32, place_ref.shape, 0), columns)


def shift_columns(value, step, columns, place):
    moved = pltpu.roll(value, step % value.shape[0], 0)
    return jnp.where(place == (0 if step == 1 else columns - 1), 0.0, moved)


def join_columns(parts, step, columns, place):
    channels = parts.shape[1] // 3
    return (
        parts[:, channels : 2 * channels]
        + shift_columns(parts[:, :channels], step, columns, place)
        + shift_columns(parts[:, 2 * channels :], -step, columns, place)
    )


def spread_columns(hg, columns, place):
    value = hg.astype(f32)
    return jnp.concatenate(
        [
            shift_columns(value, -1, columns, place).astype(bf16),
            hg,
            shift_columns(value, 1, columns, place).astype(bf16),
        ],
        axis=1,
    )


def fill_rows(patch, a, plane, columns, mirror):
    cells, channels = plane.shape
    edge = jnp.zeros((columns, channels), plane.dtype)
    for b in range(3):
        at = a * 3 + b
        step = 1 - b if mirror else b - 1
        if step == 0:
            patch[at] = plane[...]
        elif step < 0:
            patch[at, pl.ds(0, columns), :] = edge
            patch[at, pl.ds(columns, cells - columns), :] = plane[pl.ds(0, cells - columns), :]
        else:
            patch[at, pl.ds(0, cells - columns), :] = plane[pl.ds(columns, cells - columns), :]
            patch[at, pl.ds(cells - columns, columns), :] = edge


def taps_dot(patch, wide, taps):
    return jnp.dot(
        jnp.concatenate([patch[t] for t in taps], axis=1),
        jnp.concatenate([wide[t] for t in taps], axis=0),
        preferred_element_type=f32,
    )


def clear_outside(patch, a):
    index = lax.axis_index("space")

    @pl.when(jnp.logical_or(index == 0, index == lax.axis_size("space") - 1))
    def _():
        for b in range(3):
            patch[a * 3 + b] = jnp.zeros(patch.shape[1:], patch.dtype)


def activate(summed, pulled, hidden_ref, hg_ref):
    hidden_ref[0] = jnp.where(summed > 0, summed, leak_slope * summed).astype(bf16)
    hg_ref[0] = (pulled * jnp.where(summed > 0, 1.0, leak_slope)).astype(bf16)


def kernel_grads(columns, place, patch, hidden_ref, hg_ref, fg, rows_ref, before_ref):
    channels = hidden_ref.shape[2]
    width = fg.shape[1]
    wide_hg = spread_columns(hg_ref[0], columns, place)
    for ab in range(9):
        block = lax.dot_general(patch[ab], wide_hg, TN, preferred_element_type=f32)
        for e in range(3):
            rows = pl.ds((ab * 3 + e) * channels, channels)
            value = block[:, e * channels : (e + 1) * channels]
            rows_ref[rows, :] = value if before_ref is None else value + before_ref[rows, :]
    mixed = lax.dot_general(hidden_ref[0], fg, TN, preferred_element_type=f32)
    parts = width // channels
    for j in range(parts):
        rows = pl.ds(27 * channels + j, channels, stride=parts)
        value = mixed[:, j * channels : (j + 1) * channels]
        rows_ref[rows, :] = value if before_ref is None else value + before_ref[rows, :]


def inner_kernel(columns, place_ref, w_hbm, mix_hbm, fg_hbm, near_ref, far_ref,
                 near_part, far_part, near_pulled, far_pulled, wide, mix_ref, fg_ref,
                 near_patch, far_patch, sems):
    channels = near_ref.shape[2]
    parity, side = turn()
    copies = [
        pltpu.make_async_copy(fg_hbm, fg_ref, sems.at[0]),
        pltpu.make_async_copy(mix_hbm, mix_ref, sems.at[1]),
    ]
    for e in range(3):
        copies.append(pltpu.make_async_copy(
            w_hbm.at[:, e], wide.at[:, :, pl.ds(e * channels, channels)], sems.at[2 + e]
        ))
    for copy in copies:
        copy.start()
    fill_rows(near_patch, 1, near_ref.at[0], columns, False)
    fill_rows(near_patch, side, far_ref.at[0], columns, False)
    fill_rows(far_patch, 1, far_ref.at[0], columns, False)
    fill_rows(far_patch, 2 - side, near_ref.at[0], columns, False)
    for copy in copies[:2]:
        copy.wait()
    near_pulled[...] = lax.dot_general(fg_ref[1 - parity], mix_ref[...], NT, preferred_element_type=f32)
    far_pulled[...] = lax.dot_general(fg_ref[parity], mix_ref[...], NT, preferred_element_type=f32)
    for copy in copies[2:]:
        copy.wait()
    for part, patch, a in ((near_part, near_patch, side), (far_part, far_patch, 2 - side)):
        taps = [3, 4, 5] + [a * 3 + b for b in range(3)]
        part[...] = join_columns(taps_dot(patch, wide, taps), 1, columns, place_ref[...])


def finish_plane(columns, place, patch, a, wide, part_ref, pulled_ref, fg, before_ref, hidden_ref, hg_ref, rows_ref):
    taps = [a * 3 + b for b in range(3)]
    summed = part_ref[...] + join_columns(taps_dot(patch, wide, taps), 1, columns, place)
    activate(summed, pulled_ref[...], hidden_ref, hg_ref)
    kernel_grads(columns, place, patch, hidden_ref, hg_ref, fg, rows_ref, before_ref)


def near_kernel(columns, place_ref, near_ref, far_ref, pair_ref, wide, fg_ref, part_ref, pulled_ref,
                hidden_ref, hg_ref, rows_ref, patch):
    parity, side = turn()
    fill_rows(patch, 2 - side, pair_ref.at[0], columns, False)
    fill_rows(patch, 1, near_ref.at[0], columns, False)
    fill_rows(patch, side, far_ref.at[0], columns, False)
    finish_plane(columns, place_ref[...], patch, 2 - side, wide, part_ref, pulled_ref, fg_ref[1 - parity], None,
                 hidden_ref, hg_ref, rows_ref)


def far_kernel(columns, order, place_ref, near_ref, far_ref, cross_ref, wide, fg_ref, part_ref, pulled_ref, before_ref,
               near_hg,
               hidden_ref, hg_ref, grads_ref, patch, rows_ref):
    parity, side = turn()
    fill_rows(patch, side, cross_ref.at[0], columns, False)
    clear_outside(patch, side)
    fill_rows(patch, 1, far_ref.at[0], columns, False)
    fill_rows(patch, 2 - side, near_ref.at[0], columns, False)
    finish_plane(columns, place_ref[...], patch, side, wide, part_ref, pulled_ref, fg_ref[parity], before_ref,
                 hidden_ref, hg_ref, rows_ref)
    if order is None:
        grads_ref[...] = rows_ref[...].astype(bf16)
    else:
        piece = grads_ref.shape[1]
        spots = order()
        for k, spot in enumerate(spots):
            grads_ref[spot] = rows_ref[pl.ds(k * piece, piece), :].astype(bf16)
        for spot, first, rows in runs_of(near_hg.shape[1], piece):
            grads_ref[len(spots) + spot, pl.ds(0, rows), :] = near_hg[0, pl.ds(first, rows), :]


def runs_of(cells, piece):
    step = piece // 16 * 16
    return [(spot, first, min(step, cells - first)) for spot, first in enumerate(range(0, cells, step))]


def split_kernel(start, kept_ref, came_ref, own_ref, *out_refs):
    lot = own_ref.shape[0]
    for chip in range(len(out_refs) + 1):
        for i in range(lot):
            at = chip * lot + i
            value = kept_ref[start + at].astype(f32) + came_ref[at].astype(f32)
            if chip == 0:
                own_ref[i] = value
            else:
                out_refs[chip - 1][i] = value.astype(bf16)


def gather_kernel(keeps, after_ref, own_ref, *refs):
    lot = own_ref.shape[0]
    came, out = refs[: len(refs) - lot], refs[len(refs) - lot :]
    for i in range(lot):
        value = own_ref[i]
        for ref in came:
            value = value + ref[i].astype(f32)
        out[i][...] = value if keeps and i == 0 else value.astype(bf16)


def backward_kernel(columns, place_ref, near_ref, far_ref, pair_ref, cross_ref, wide, mix_ref, near_hidden, far_hidden,
                    features_ref, input_ref, near_patch, far_patch, pair_plane):
    cells, channels = near_ref.shape[1:]
    if pair_ref.shape[1] == cells:
        pair_plane[...] = pair_ref[0]
    else:
        spots = runs_of(cells, pair_ref.shape[1])
        start = pair_ref.shape[0] - len(spots)
        for spot, first, rows in spots:
            pair_plane[pl.ds(first, rows), :] = pair_ref[start + spot, pl.ds(0, rows), :]
    parity, side = turn()
    features_ref[1 - parity] = jnp.dot(near_hidden[0], mix_ref[...], preferred_element_type=f32).astype(bf16)
    features_ref[parity] = jnp.dot(far_hidden[0], mix_ref[...], preferred_element_type=f32).astype(bf16)
    fill_rows(near_patch, side, pair_plane, columns, True)
    fill_rows(near_patch, 1, near_ref.at[0], columns, True)
    fill_rows(near_patch, 2 - side, far_ref.at[0], columns, True)
    fill_rows(far_patch, side, near_ref.at[0], columns, True)
    fill_rows(far_patch, 1, far_ref.at[0], columns, True)
    fill_rows(far_patch, 2 - side, cross_ref.at[0], columns, True)
    clear_outside(far_patch, 2 - side)
    for patch, plane in ((near_patch, 1 - parity), (far_patch, parity)):
        parts = jnp.zeros((near_ref.shape[1], 3 * channels), f32)
        for first in range(0, 9, 2):
            taps = range(first, min(first + 2, 9))
            block = jnp.concatenate(
                [
                    jnp.concatenate([wide[t, :, e * channels : (e + 1) * channels] for e in range(3)], axis=0)
                    for t in taps
                ],
                axis=1,
            )
            parts = parts + lax.dot_general(
                jnp.concatenate([patch[t] for t in taps], axis=1), block, NT, preferred_element_type=f32
            )
        input_ref[plane] = join_columns(parts, -1, columns, place_ref[...]).astype(bf16)


def digits_of(count):
    digits = []
    while count > 1:
        for radix in (2, 3, 5, 7, count) if not digits else (4, 2, 3, 5, 7, count):
            if count % radix == 0:
                digits.append(radix)
                count //= radix
                break
    return digits


def stages_of(axis, digits):
    stages, stride = [], 1
    for radix in digits:
        stages.append((axis, stride, radix))
        stride *= radix
    return stages


def apart(digit, mine, radix):
    if radix & (radix - 1) == 0:
        return lax.bitwise_xor(mine, digit)
    return lax.rem(digit - mine + radix, radix)


def send(value, stage, k):
    axis, stride, radix = stage
    pairs = []
    for i in range(lax.axis_size(axis)):
        digit = i // stride % radix
        other = digit ^ k if radix & (radix - 1) == 0 else (digit + k) % radix
        pairs.append((i, i + (other - digit) * stride))
    return lax.ppermute(value, axis, pairs)


def swaps(start, count):
    found = []
    for i in range(start, count + start, 2):
        found += [(i, (i + 1) % count), ((i + 1) % count, i)]
    return found


def shards(universes, conv_weight, mix_weight, feature_grad):
    channels = conv_weight.shape[1]
    width = mix_weight.shape[1]
    planes, map_rows, columns = universes.shape[1:4]
    if planes != 2 or lax.axis_size("space") % 2:
        raise ValueError("slab shape")
    cells = map_rows * columns
    group_count, slab_count = lax.axis_size("dp"), lax.axis_size("space")
    devices = group_count * slab_count
    space_digits = digits_of(slab_count)
    dp_digits = [4] if group_count == 4 else digits_of(group_count)
    stages = stages_of("space", space_digits) + stages_of("dp", dp_digits)

    x = universes.reshape(planes, cells, channels)
    fg = feature_grad.reshape(planes, cells, width)
    weights = conv_weight.reshape(9, 3, channels, channels)
    pair_swaps, cross_swaps = swaps(0, slab_count), swaps(1, slab_count)

    parity = lax.rem(lax.axis_index("space"), 2)
    x_near = lax.dynamic_slice_in_dim(x, 1 - parity, 1, 0)
    x_far = lax.dynamic_slice_in_dim(x, parity, 1, 0)
    x_cross = lax.ppermute(x_far, "space", cross_swaps)
    x_pair = lax.ppermute(x_near, "space", pair_swaps)

    total_rows = 27 * channels + channels * width // channels
    share = (total_rows * channels + devices - 1) // devices
    lots = (
        share * devices == total_rows * channels
        and share % channels == 0
        and len(stages) == 3
        and stages[0][2] == 2
        and stages[1][2] == 4
        and stages[2][2] == 4
    )
    if lots:
        piece = share // channels
        chips, groups = stages[1][2], stages[2][2]
        lot = groups // 2
        grads_shape = (devices + len(runs_of(cells, piece)), piece, channels)

        def order():
            def relative(stage):
                axis, stride, radix = stage
                mine = lax.rem(lax.div(lax.axis_index(axis), stride), radix)
                return [apart(digit, mine, radix) for digit in range(radix)]

            cores = [core * (2 * chips * lot) for core in relative(stages[0])]
            here = lax.rem(lax.div(lax.axis_index("space"), 2), 4)
            turned_round = jnp.logical_or(here == 1, here == 2)
            chip_spots = []
            for chip in relative(stages[1]):
                side = jnp.logical_or(chip == 1, chip == 2)
                chip_spots.append(lax.select(jnp.logical_and(turned_round, side), 3 - chip, chip) * lot)
            mine = lax.axis_index("dp")
            late = lax.div(mine, lot)
            group_spots = []
            for group in relative(stages[2]):
                near = 1 - lax.div(group, lot)
                group_spots.append(near * (chips * lot) + lax.rem(group + (1 - near) * late, lot))
            spots = []
            for k in range(devices):
                group, place = divmod(k, slab_count)
                chip, core = divmod(place, 2)
                spots.append(cores[core] + chip_spots[chip] + group_spots[group])
            return spots
    else:
        grads_shape = (total_rows, channels)
        order = None

    def like(*shape, dtype=bf16):
        return jax.ShapeDtypeStruct(shape, dtype)

    def params(mebibytes):
        return pltpu.CompilerParams(vmem_limit_bytes=mebibytes * 1024 * 1024)

    def cost(blocks, read):
        return pl.CostEstimate(
            flops=2 * cells * channels * channels * blocks, bytes_accessed=read, transcendentals=0
        )

    plane = like(1, cells, channels)
    plane_sum = like(cells, channels, dtype=f32)
    patch = pltpu.VMEM((9, cells, channels), bf16)
    place = pl.pallas_call(
        functools.partial(columns_kernel, columns),
        out_shape=like(cells, channels, dtype=jnp.int32),
        out_specs=VMEM,
        compiler_params=params(4),
        cost_estimate=cost(100, 8_000_000),
        name="columns_of_cells",
    )()
    near_part, far_part, near_pulled, far_pulled, wide, mix_near, fg_near = pl.pallas_call(
        functools.partial(inner_kernel, columns),
        out_shape=(plane_sum,) * 4
        + (like(9, channels, 3 * channels), like(*mix_weight.shape), like(*fg.shape)),
        in_specs=[VMEM] + [HBM] * 3 + [VMEM] * 2,
        out_specs=(VMEM,) * 7,
        scratch_shapes=[patch, patch, pltpu.SemaphoreType.DMA((5,))],
        compiler_params=params(16),
        cost_estimate=cost(44, 2_000_000),
        name="inner_taps",
    )(place, weights, mix_weight, fg, x_near, x_far)
    near_hidden, near_hg, near_rows = pl.pallas_call(
        functools.partial(near_kernel, columns),
        out_shape=(plane, plane, like(total_rows, channels, dtype=f32)),
        in_specs=[VMEM] * 8,
        out_specs=(VMEM,) * 3,
        scratch_shapes=[patch],
        compiler_params=params(16),
        cost_estimate=cost(38, 3_000_000),
        name="near_plane",
    )(place, x_near, x_far, x_pair, wide, fg_near, near_part, near_pulled)
    far_hidden, far_hg, grads = pl.pallas_call(
        functools.partial(far_kernel, columns, order),
        out_shape=(plane, plane, like(*grads_shape)),
        in_specs=[VMEM] * 10,
        out_specs=(VMEM,) * 3,
        scratch_shapes=[patch, pltpu.VMEM((total_rows, channels), f32)],
        compiler_params=params(16),
        cost_estimate=cost(38, 3_000_000),
        name="far_plane",
    )(place, x_near, x_far, x_cross, wide, fg_near, far_part, far_pulled, near_rows, near_hg)

    hg_cross = lax.ppermute(far_hg, "space", cross_swaps)
    if lots:
        size = devices // 4
        first = send(grads[2 * size : 3 * size], stages[0], 1)
        second = send(grads[3 * size :], stages[0], 1)
        hg_pair = second
    else:
        hg_pair = lax.ppermute(near_hg, "space", pair_swaps)
    features, input_grad = pl.pallas_call(
        functools.partial(backward_kernel, columns),
        out_shape=(like(planes, cells, width), like(planes, cells, channels)),
        in_specs=[VMEM] * 9,
        out_specs=(VMEM, VMEM),
        scratch_shapes=[patch, patch, pltpu.VMEM((cells, channels), bf16)],
        compiler_params=params(16),
        cost_estimate=cost(58, 2_000_000),
        name="features_and_input_grad",
    )(place, near_hg, far_hg, hg_pair, hg_cross, wide, mix_near, near_hidden, far_hidden)

    if lots:
        arrived = []
        for start, came, near in ((0, first, False), (size, second, True)):
            own, *others = pl.pallas_call(
                functools.partial(split_kernel, start),
                out_shape=[like(lot, piece, channels, dtype=f32)] + [like(lot, piece, channels)] * (chips - 1),
                in_specs=[VMEM, VMEM],
                out_specs=[VMEM] * chips,
                compiler_params=params(8),
                name="sum_of_core_pair",
            )(grads, came)
            came = [
                lax.ppermute(
                    others[k], "space", [(2 * a + core, 2 * b + core) for a, b in CHIP_ROUNDS[k] for core in range(2)]
                )
                for k in (2, 1, 0)
            ]
            parts = pl.pallas_call(
                functools.partial(gather_kernel, near),
                out_shape=[like(piece, channels, dtype=f32 if near and i == 0 else bf16) for i in range(lot)],
                in_specs=[pl.BlockSpec(memory_space=pl.ANY)] + [VMEM] * chips,
                out_specs=[VMEM] * lot,
                compiler_params=params(8),
                name="sum_of_chips",
            )(hg_cross, own, *came)
            if near:
                arrived += [parts[0], send(parts[1], stages[2], 1).astype(f32)]
            else:
                arrived += [lax.ppermute(part, "dp", pairs).astype(f32) for part, pairs in zip(parts, FAR_ROUNDS)]
        total = sum(arrived[1:], arrived[0])
    else:
        flat = grads.reshape(-1)
        flat = jnp.pad(flat, (0, share * devices - flat.size))
        held = flat.reshape(dp_digits[::-1] + space_digits[::-1] + [share])
        places = {}
        for spot, stage in enumerate(stages_of("dp", dp_digits)[::-1] + stages_of("space", space_digits)[::-1]):
            places[stage] = spot
            mine = lax.rem(lax.axis_index(stage[0]) // stage[1], stage[2])
            held = jnp.take(held, apart(jnp.arange(stage[2]), mine, stage[2]), axis=spot)
        parts = jnp.transpose(held, [places[stage] for stage in stages] + [len(stages)])
        for stage in stages:
            total = parts[0].astype(f32)
            for term in [send(parts[k], stage, k) for k in range(1, stage[2])]:
                total = total + term.astype(f32)
            parts = total.astype(bf16)
    weight_grads = (total / devices).reshape(-1)
    return (features.reshape(feature_grad.shape), input_grad.reshape(universes.shape), weight_grads)


def solution(mesh):
    return jax.shard_map(
        shards,
        mesh=mesh,
        in_specs=(P("dp", "space", None, None, None), P(), P(), P("dp", "space", None, None, None)),
        out_specs=(
            P("dp", "space", None, None, None),
            P("dp", "space", None, None, None),
            P(("dp", "space")),
        ),
        check_vma=False,
    )
```

```python
import functools

import jax
import jax.numpy as jnp
from jax import lax
from jax.experimental import pallas as pl
from jax.experimental.pallas import tpu as pltpu
from jax.sharding import PartitionSpec as P

leak_slope = 0.3
bf16 = jnp.bfloat16
f32 = jnp.float32
NT = (((1,), (1,)), ((), ()))
TN = (((0,), (0,)), ((), ()))
VMEM = pl.BlockSpec(memory_space=pltpu.VMEM)
HBM = pl.BlockSpec(memory_space=pltpu.HBM)

CHIP_ROUNDS = (
    ((0, 1), (1, 3), (3, 2), (2, 0)),
    ((0, 2), (2, 3), (3, 1), (1, 0)),
    ((0, 3), (3, 0), (1, 2), (2, 1)),
)
FAR_ROUNDS = (((0, 2), (2, 1), (1, 3), (3, 0)), ((0, 3), (3, 1), (1, 2), (2, 0)))


def turn():
    parity = lax.rem(lax.axis_index("space"), 2)
    return parity, 2 * parity


def columns_kernel(columns, place_ref):
    place_ref[...] = lax.rem(lax.broadcasted_iota(jnp.int32, place_ref.shape, 0), columns)


def shift_columns(value, step, columns, place):
    moved = pltpu.roll(value, step % value.shape[0], 0)
    return jnp.where(place == (0 if step == 1 else columns - 1), 0.0, moved)


def join_columns(parts, step, columns, place):
    channels = parts.shape[1] // 3
    return (
        parts[:, channels : 2 * channels]
        + shift_columns(parts[:, :channels], step, columns, place)
        + shift_columns(parts[:, 2 * channels :], -step, columns, place)
    )


def spread_columns(hg, columns, place):
    value = hg.astype(f32)
    return jnp.concatenate(
        [
            shift_columns(value, -1, columns, place).astype(bf16),
            hg,
            shift_columns(value, 1, columns, place).astype(bf16),
        ],
        axis=1,
    )


def fill_rows(patch, a, plane, columns, mirror):
    cells, channels = plane.shape
    edge = jnp.zeros((columns, channels), plane.dtype)
    for b in range(3):
        at = a * 3 + b
        step = 1 - b if mirror else b - 1
        if step == 0:
            patch[at] = plane[...]
        elif step < 0:
            patch[at, pl.ds(0, columns), :] = edge
            patch[at, pl.ds(columns, cells - columns), :] = plane[pl.ds(0, cells - columns), :]
        else:
            patch[at, pl.ds(0, cells - columns), :] = plane[pl.ds(columns, cells - columns), :]
            patch[at, pl.ds(cells - columns, columns), :] = edge


def taps_dot(patch, wide, taps):
    return jnp.dot(
        jnp.concatenate([patch[t] for t in taps], axis=1),
        jnp.concatenate([wide[t] for t in taps], axis=0),
        preferred_element_type=f32,
    )


def clear_outside(patch, a):
    index = lax.axis_index("space")

    @pl.when(jnp.logical_or(index == 0, index == lax.axis_size("space") - 1))
    def _():
        for b in range(3):
            patch[a * 3 + b] = jnp.zeros(patch.shape[1:], patch.dtype)


def activate(summed, pulled, hidden_ref, hg_ref):
    hidden_ref[0] = jnp.where(summed > 0, summed, leak_slope * summed).astype(bf16)
    hg_ref[0] = (pulled * jnp.where(summed > 0, 1.0, leak_slope)).astype(bf16)


def kernel_grads(columns, place, patch, hidden_ref, hg_ref, fg, rows_ref, before_ref):
    channels = hidden_ref.shape[2]
    width = fg.shape[1]
    wide_hg = spread_columns(hg_ref[0], columns, place)
    for ab in range(9):
        block = lax.dot_general(patch[ab], wide_hg, TN, preferred_element_type=f32)
        for e in range(3):
            rows = pl.ds((ab * 3 + e) * channels, channels)
            value = block[:, e * channels : (e + 1) * channels]
            rows_ref[rows, :] = value if before_ref is None else value + before_ref[rows, :]
    mixed = lax.dot_general(hidden_ref[0], fg, TN, preferred_element_type=f32)
    parts = width // channels
    for j in range(parts):
        rows = pl.ds(27 * channels + j, channels, stride=parts)
        value = mixed[:, j * channels : (j + 1) * channels]
        rows_ref[rows, :] = value if before_ref is None else value + before_ref[rows, :]


def inner_kernel(columns, place_ref, w_hbm, mix_hbm, fg_hbm, near_ref, far_ref,
                 near_part, far_part, near_pulled, far_pulled, wide, mix_ref, fg_ref,
                 near_patch, far_patch, sems):
    channels = near_ref.shape[2]
    parity, side = turn()
    copies = [
        pltpu.make_async_copy(fg_hbm, fg_ref, sems.at[0]),
        pltpu.make_async_copy(mix_hbm, mix_ref, sems.at[1]),
    ]
    for e in range(3):
        copies.append(pltpu.make_async_copy(
            w_hbm.at[:, e], wide.at[:, :, pl.ds(e * channels, channels)], sems.at[2 + e]
        ))
    for copy in copies:
        copy.start()
    fill_rows(near_patch, 1, near_ref.at[0], columns, False)
    fill_rows(near_patch, side, far_ref.at[0], columns, False)
    fill_rows(far_patch, 1, far_ref.at[0], columns, False)
    fill_rows(far_patch, 2 - side, near_ref.at[0], columns, False)
    for copy in copies[:2]:
        copy.wait()
    near_pulled[...] = lax.dot_general(fg_ref[1 - parity], mix_ref[...], NT, preferred_element_type=f32)
    far_pulled[...] = lax.dot_general(fg_ref[parity], mix_ref[...], NT, preferred_element_type=f32)
    for copy in copies[2:]:
        copy.wait()
    for part, patch, a in ((near_part, near_patch, side), (far_part, far_patch, 2 - side)):
        taps = [3, 4, 5] + [a * 3 + b for b in range(3)]
        part[...] = join_columns(taps_dot(patch, wide, taps), 1, columns, place_ref[...])


def finish_plane(columns, place, patch, a, wide, part_ref, pulled_ref, fg, before_ref, hidden_ref, hg_ref, rows_ref):
    taps = [a * 3 + b for b in range(3)]
    summed = part_ref[...] + join_columns(taps_dot(patch, wide, taps), 1, columns, place)
    activate(summed, pulled_ref[...], hidden_ref, hg_ref)
    kernel_grads(columns, place, patch, hidden_ref, hg_ref, fg, rows_ref, before_ref)


def near_kernel(columns, place_ref, near_ref, far_ref, pair_ref, wide, fg_ref, part_ref, pulled_ref,
                hidden_ref, hg_ref, rows_ref, patch):
    parity, side = turn()
    fill_rows(patch, 2 - side, pair_ref.at[0], columns, False)
    fill_rows(patch, 1, near_ref.at[0], columns, False)
    fill_rows(patch, side, far_ref.at[0], columns, False)
    finish_plane(columns, place_ref[...], patch, 2 - side, wide, part_ref, pulled_ref, fg_ref[1 - parity], None,
                 hidden_ref, hg_ref, rows_ref)


def far_kernel(columns, order, place_ref, near_ref, far_ref, cross_ref, wide, fg_ref, part_ref, pulled_ref, before_ref,
               near_hg,
               hidden_ref, hg_ref, grads_ref, patch, rows_ref):
    parity, side = turn()
    fill_rows(patch, side, cross_ref.at[0], columns, False)
    clear_outside(patch, side)
    fill_rows(patch, 1, far_ref.at[0], columns, False)
    fill_rows(patch, 2 - side, near_ref.at[0], columns, False)
    finish_plane(columns, place_ref[...], patch, side, wide, part_ref, pulled_ref, fg_ref[parity], before_ref,
                 hidden_ref, hg_ref, rows_ref)
    if order is None:
        grads_ref[...] = rows_ref[...].astype(bf16)
    else:
        piece = grads_ref.shape[1]
        spots = order()
        for k, spot in enumerate(spots):
            grads_ref[spot] = rows_ref[pl.ds(k * piece, piece), :].astype(bf16)
        for spot, first, rows in runs_of(near_hg.shape[1], piece):
            grads_ref[len(spots) + spot, pl.ds(0, rows), :] = near_hg[0, pl.ds(first, rows), :]


def runs_of(cells, piece):
    step = piece // 16 * 16
    return [(spot, first, min(step, cells - first)) for spot, first in enumerate(range(0, cells, step))]


def split_kernel(start, kept_ref, came_ref, own_ref, *out_refs):
    lot = own_ref.shape[0]
    for chip in range(len(out_refs) + 1):
        for i in range(lot):
            at = chip * lot + i
            value = kept_ref[start + at].astype(f32) + came_ref[at].astype(f32)
            if chip == 0:
                own_ref[i] = value
            else:
                out_refs[chip - 1][i] = value.astype(bf16)


def gather_kernel(keeps, after_ref, own_ref, *refs):
    lot = own_ref.shape[0]
    came, out = refs[: len(refs) - lot], refs[len(refs) - lot :]
    for i in range(lot):
        value = own_ref[i]
        for ref in came:
            value = value + ref[i].astype(f32)
        out[i][...] = value if keeps and i == 0 else value.astype(bf16)


def backward_kernel(columns, place_ref, near_ref, far_ref, pair_ref, cross_ref, wide, mix_ref, near_hidden, far_hidden,
                    features_ref, input_ref, near_patch, far_patch, pair_plane):
    cells, channels = near_ref.shape[1:]
    if pair_ref.shape[1] == cells:
        pair_plane[...] = pair_ref[0]
    else:
        spots = runs_of(cells, pair_ref.shape[1])
        start = pair_ref.shape[0] - len(spots)
        for spot, first, rows in spots:
            pair_plane[pl.ds(first, rows), :] = pair_ref[start + spot, pl.ds(0, rows), :]
    parity, side = turn()
    features_ref[1 - parity] = jnp.dot(near_hidden[0], mix_ref[...], preferred_element_type=f32).astype(bf16)
    features_ref[parity] = jnp.dot(far_hidden[0], mix_ref[...], preferred_element_type=f32).astype(bf16)
    fill_rows(near_patch, side, pair_plane, columns, True)
    fill_rows(near_patch, 1, near_ref.at[0], columns, True)
    fill_rows(near_patch, 2 - side, far_ref.at[0], columns, True)
    fill_rows(far_patch, side, near_ref.at[0], columns, True)
    fill_rows(far_patch, 1, far_ref.at[0], columns, True)
    fill_rows(far_patch, 2 - side, cross_ref.at[0], columns, True)
    clear_outside(far_patch, 2 - side)
    for patch, plane in ((near_patch, 1 - parity), (far_patch, parity)):
        parts = jnp.zeros((near_ref.shape[1], 3 * channels), f32)
        for first in range(0, 9, 2):
            taps = range(first, min(first + 2, 9))
            block = jnp.concatenate(
                [
                    jnp.concatenate([wide[t, :, e * channels : (e + 1) * channels] for e in range(3)], axis=0)
                    for t in taps
                ],
                axis=1,
            )
            parts = parts + lax.dot_general(
                jnp.concatenate([patch[t] for t in taps], axis=1), block, NT, preferred_element_type=f32
            )
        input_ref[plane] = join_columns(parts, -1, columns, place_ref[...]).astype(bf16)


def digits_of(count):
    digits = []
    while count > 1:
        for radix in (2, 3, 5, 7, count) if not digits else (4, 2, 3, 5, 7, count):
            if count % radix == 0:
                digits.append(radix)
                count //= radix
                break
    return digits


def stages_of(axis, digits):
    stages, stride = [], 1
    for radix in digits:
        stages.append((axis, stride, radix))
        stride *= radix
    return stages


def apart(digit, mine, radix):
    if radix & (radix - 1) == 0:
        return lax.bitwise_xor(mine, digit)
    return lax.rem(digit - mine + radix, radix)


def send(value, stage, k):
    axis, stride, radix = stage
    pairs = []
    for i in range(lax.axis_size(axis)):
        digit = i // stride % radix
        other = digit ^ k if radix & (radix - 1) == 0 else (digit + k) % radix
        pairs.append((i, i + (other - digit) * stride))
    return lax.ppermute(value, axis, pairs)


def swaps(start, count):
    found = []
    for i in range(start, count + start, 2):
        found += [(i, (i + 1) % count), ((i + 1) % count, i)]
    return found


def shards(universes, conv_weight, mix_weight, feature_grad):
    channels = conv_weight.shape[1]
    width = mix_weight.shape[1]
    planes, map_rows, columns = universes.shape[1:4]
    if planes != 2 or lax.axis_size("space") % 2:
        raise ValueError("slab shape")
    cells = map_rows * columns
    group_count, slab_count = lax.axis_size("dp"), lax.axis_size("space")
    devices = group_count * slab_count
    space_digits = digits_of(slab_count)
    dp_digits = [4] if group_count == 4 else digits_of(group_count)
    stages = stages_of("space", space_digits) + stages_of("dp", dp_digits)

    x = universes.reshape(planes, cells, channels)
    fg = feature_grad.reshape(planes, cells, width)
    weights = conv_weight.reshape(9, 3, channels, channels)
    pair_swaps, cross_swaps = swaps(0, slab_count), swaps(1, slab_count)

    parity = lax.rem(lax.axis_index("space"), 2)
    x_near = lax.dynamic_slice_in_dim(x, 1 - parity, 1, 0)
    x_far = lax.dynamic_slice_in_dim(x, parity, 1, 0)
    x_cross = lax.ppermute(x_far, "space", cross_swaps)
    x_pair = lax.ppermute(x_near, "space", pair_swaps)

    total_rows = 27 * channels + channels * width // channels
    share = (total_rows * channels + devices - 1) // devices
    lots = (
        share * devices == total_rows * channels
        and share % channels == 0
        and len(stages) == 3
        and stages[0][2] == 2
        and stages[1][2] == 4
        and stages[2][2] == 4
    )
    if lots:
        piece = share // channels
        chips, groups = stages[1][2], stages[2][2]
        lot = groups // 2
        grads_shape = (devices + len(runs_of(cells, piece)), piece, channels)

        def order():
            def relative(stage):
                axis, stride, radix = stage
                mine = lax.rem(lax.div(lax.axis_index(axis), stride), radix)
                return [apart(digit, mine, radix) for digit in range(radix)]

            cores = [core * (2 * chips * lot) for core in relative(stages[0])]
            here = lax.rem(lax.div(lax.axis_index("space"), 2), 4)
            turned_round = jnp.logical_or(here == 1, here == 2)
            chip_spots = []
            for chip in relative(stages[1]):
                side = jnp.logical_or(chip == 1, chip == 2)
                chip_spots.append(lax.select(jnp.logical_and(turned_round, side), 3 - chip, chip) * lot)
            mine = lax.axis_index("dp")
            late = lax.div(mine, lot)
            group_spots = []
            for group in relative(stages[2]):
                near = 1 - lax.div(group, lot)
                group_spots.append(near * (chips * lot) + lax.rem(group + (1 - near) * late, lot))
            spots = []
            for k in range(devices):
                group, place = divmod(k, slab_count)
                chip, core = divmod(place, 2)
                spots.append(cores[core] + chip_spots[chip] + group_spots[group])
            return spots
    else:
        grads_shape = (total_rows, channels)
        order = None

    def like(*shape, dtype=bf16):
        return jax.ShapeDtypeStruct(shape, dtype)

    def params(mebibytes):
        return pltpu.CompilerParams(vmem_limit_bytes=mebibytes * 1024 * 1024)

    def cost(blocks, read):
        return pl.CostEstimate(
            flops=2 * cells * channels * channels * blocks, bytes_accessed=read, transcendentals=0
        )

    plane = like(1, cells, channels)
    plane_sum = like(cells, channels, dtype=f32)
    patch = pltpu.VMEM((9, cells, channels), bf16)
    place = pl.pallas_call(
        functools.partial(columns_kernel, columns),
        out_shape=like(cells, channels, dtype=jnp.int32),
        out_specs=VMEM,
        compiler_params=params(4),
        cost_estimate=cost(100, 8_000_000),
        name="columns_of_cells",
    )()
    near_part, far_part, near_pulled, far_pulled, wide, mix_near, fg_near = pl.pallas_call(
        functools.partial(inner_kernel, columns),
        out_shape=(plane_sum,) * 4
        + (like(9, channels, 3 * channels), like(*mix_weight.shape), like(*fg.shape)),
        in_specs=[VMEM] + [HBM] * 3 + [VMEM] * 2,
        out_specs=(VMEM,) * 7,
        scratch_shapes=[patch, patch, pltpu.SemaphoreType.DMA((5,))],
        compiler_params=params(16),
        cost_estimate=cost(44, 2_000_000),
        name="inner_taps",
    )(place, weights, mix_weight, fg, x_near, x_far)
    near_hidden, near_hg, near_rows = pl.pallas_call(
        functools.partial(near_kernel, columns),
        out_shape=(plane, plane, like(total_rows, channels, dtype=f32)),
        in_specs=[VMEM] * 8,
        out_specs=(VMEM,) * 3,
        scratch_shapes=[patch],
        compiler_params=params(16),
        cost_estimate=cost(38, 3_000_000),
        name="near_plane",
    )(place, x_near, x_far, x_pair, wide, fg_near, near_part, near_pulled)
    far_hidden, far_hg, grads = pl.pallas_call(
        functools.partial(far_kernel, columns, order),
        out_shape=(plane, plane, like(*grads_shape)),
        in_specs=[VMEM] * 10,
        out_specs=(VMEM,) * 3,
        scratch_shapes=[patch, pltpu.VMEM((total_rows, channels), f32)],
        compiler_params=params(16),
        cost_estimate=cost(38, 3_000_000),
        name="far_plane",
    )(place, x_near, x_far, x_cross, wide, fg_near, far_part, far_pulled, near_rows, near_hg)

    hg_cross = lax.ppermute(far_hg, "space", cross_swaps)
    if lots:
        size = devices // 4
        first = send(grads[2 * size : 3 * size], stages[0], 1)
        second = send(grads[3 * size :], stages[0], 1)
        hg_pair = second
    else:
        hg_pair = lax.ppermute(near_hg, "space", pair_swaps)
    features, input_grad = pl.pallas_call(
        functools.partial(backward_kernel, columns),
        out_shape=(like(planes, cells, width), like(planes, cells, channels)),
        in_specs=[VMEM] * 9,
        out_specs=(VMEM, VMEM),
        scratch_shapes=[patch, patch, pltpu.VMEM((cells, channels), bf16)],
        compiler_params=params(16),
        cost_estimate=cost(58, 2_000_000),
        name="features_and_input_grad",
    )(place, near_hg, far_hg, hg_pair, hg_cross, wide, mix_near, near_hidden, far_hidden)

    if lots:
        arrived = []
        for start, came, near in ((0, first, False), (size, second, True)):
            own, *others = pl.pallas_call(
                functools.partial(split_kernel, start),
                out_shape=[like(lot, piece, channels, dtype=f32)] + [like(lot, piece, channels)] * (chips - 1),
                in_specs=[VMEM, VMEM],
                out_specs=[VMEM] * chips,
                compiler_params=params(8),
                name="sum_of_core_pair",
            )(grads, came)
            came = [
                lax.ppermute(
                    others[k], "space", [(2 * a + core, 2 * b + core) for a, b in CHIP_ROUNDS[k] for core in range(2)]
                )
                for k in (1, 2, 0)
            ]
            parts = pl.pallas_call(
                functools.partial(gather_kernel, near),
                out_shape=[like(piece, channels, dtype=f32 if near and i == 0 else bf16) for i in range(lot)],
                in_specs=[pl.BlockSpec(memory_space=pl.ANY)] + [VMEM] * chips,
                out_specs=[VMEM] * lot,
                compiler_params=params(8),
                name="sum_of_chips",
            )(hg_cross, own, *came)
            if near:
                arrived += [parts[0], send(parts[1], stages[2], 1).astype(f32)]
            else:
                arrived += [lax.ppermute(part, "dp", pairs).astype(f32) for part, pairs in zip(parts, FAR_ROUNDS)]
        total = sum(arrived[1:], arrived[0])
    else:
        flat = grads.reshape(-1)
        flat = jnp.pad(flat, (0, share * devices - flat.size))
        held = flat.reshape(dp_digits[::-1] + space_digits[::-1] + [share])
        places = {}
        for spot, stage in enumerate(stages_of("dp", dp_digits)[::-1] + stages_of("space", space_digits)[::-1]):
            places[stage] = spot
            mine = lax.rem(lax.axis_index(stage[0]) // stage[1], stage[2])
            held = jnp.take(held, apart(jnp.arange(stage[2]), mine, stage[2]), axis=spot)
        parts = jnp.transpose(held, [places[stage] for stage in stages] + [len(stages)])
        for stage in stages:
            total = parts[0].astype(f32)
            for term in [send(parts[k], stage, k) for k in range(1, stage[2])]:
                total = total + term.astype(f32)
            parts = total.astype(bf16)
    weight_grads = (total / devices).reshape(-1)
    return (features.reshape(feature_grad.shape), input_grad.reshape(universes.shape), weight_grads)


def solution(mesh):
    return jax.shard_map(
        shards,
        mesh=mesh,
        in_specs=(P("dp", "space", None, None, None), P(), P(), P("dp", "space", None, None, None)),
        out_specs=(
            P("dp", "space", None, None, None),
            P("dp", "space", None, None, None),
            P(("dp", "space")),
        ),
        check_vma=False,
    )
```

```python
import functools

import jax
import jax.numpy as jnp
from jax import lax
from jax.experimental import pallas as pl
from jax.experimental.pallas import tpu as pltpu
from jax.sharding import PartitionSpec as P

leak_slope = 0.3
bf16 = jnp.bfloat16
f32 = jnp.float32
NT = (((1,), (1,)), ((), ()))
TN = (((0,), (0,)), ((), ()))
VMEM = pl.BlockSpec(memory_space=pltpu.VMEM)
HBM = pl.BlockSpec(memory_space=pltpu.HBM)

CHIP_ROUNDS = (
    ((0, 1), (1, 3), (3, 2), (2, 0)),
    ((0, 2), (2, 3), (3, 1), (1, 0)),
    ((0, 3), (3, 0), (1, 2), (2, 1)),
)
FAR_ROUNDS = (((0, 2), (2, 1), (1, 3), (3, 0)), ((0, 3), (3, 1), (1, 2), (2, 0)))


def turn():
    parity = lax.rem(lax.axis_index("space"), 2)
    return parity, 2 * parity


def columns_kernel(columns, place_ref):
    place_ref[...] = lax.rem(lax.broadcasted_iota(jnp.int32, place_ref.shape, 0), columns)


def shift_columns(value, step, columns, place):
    moved = pltpu.roll(value, step % value.shape[0], 0)
    return jnp.where(place == (0 if step == 1 else columns - 1), 0.0, moved)


def join_columns(parts, step, columns, place):
    channels = parts.shape[1] // 3
    return (
        parts[:, channels : 2 * channels]
        + shift_columns(parts[:, :channels], step, columns, place)
        + shift_columns(parts[:, 2 * channels :], -step, columns, place)
    )


def spread_columns(hg, columns, place):
    value = hg.astype(f32)
    return jnp.concatenate(
        [
            shift_columns(value, -1, columns, place).astype(bf16),
            hg,
            shift_columns(value, 1, columns, place).astype(bf16),
        ],
        axis=1,
    )


def fill_rows(patch, a, plane, columns, mirror):
    cells, channels = plane.shape
    edge = jnp.zeros((columns, channels), plane.dtype)
    for b in range(3):
        at = a * 3 + b
        step = 1 - b if mirror else b - 1
        if step == 0:
            patch[at] = plane[...]
        elif step < 0:
            patch[at, pl.ds(0, columns), :] = edge
            patch[at, pl.ds(columns, cells - columns), :] = plane[pl.ds(0, cells - columns), :]
        else:
            patch[at, pl.ds(0, cells - columns), :] = plane[pl.ds(columns, cells - columns), :]
            patch[at, pl.ds(cells - columns, columns), :] = edge


def taps_dot(patch, wide, taps):
    return jnp.dot(
        jnp.concatenate([patch[t] for t in taps], axis=1),
        jnp.concatenate([wide[t] for t in taps], axis=0),
        preferred_element_type=f32,
    )


def clear_outside(patch, a):
    index = lax.axis_index("space")

    @pl.when(jnp.logical_or(index == 0, index == lax.axis_size("space") - 1))
    def _():
        for b in range(3):
            patch[a * 3 + b] = jnp.zeros(patch.shape[1:], patch.dtype)


def activate(summed, pulled, hidden_ref, hg_ref):
    hidden_ref[0] = jnp.where(summed > 0, summed, leak_slope * summed).astype(bf16)
    hg_ref[0] = (pulled * jnp.where(summed > 0, 1.0, leak_slope)).astype(bf16)


def kernel_grads(columns, place, patch, hidden_ref, hg_ref, fg, rows_ref, before_ref):
    channels = hidden_ref.shape[2]
    width = fg.shape[1]
    wide_hg = spread_columns(hg_ref[0], columns, place)
    for ab in range(9):
        block = lax.dot_general(patch[ab], wide_hg, TN, preferred_element_type=f32)
        for e in range(3):
            rows = pl.ds((ab * 3 + e) * channels, channels)
            value = block[:, e * channels : (e + 1) * channels]
            rows_ref[rows, :] = value if before_ref is None else value + before_ref[rows, :]
    mixed = lax.dot_general(hidden_ref[0], fg, TN, preferred_element_type=f32)
    parts = width // channels
    for j in range(parts):
        rows = pl.ds(27 * channels + j, channels, stride=parts)
        value = mixed[:, j * channels : (j + 1) * channels]
        rows_ref[rows, :] = value if before_ref is None else value + before_ref[rows, :]


def inner_kernel(columns, place_ref, w_hbm, mix_hbm, fg_hbm, near_ref, far_ref,
                 near_part, far_part, near_pulled, far_pulled, wide, mix_ref, fg_ref,
                 near_patch, far_patch, sems):
    channels = near_ref.shape[2]
    parity, side = turn()
    copies = [
        pltpu.make_async_copy(fg_hbm, fg_ref, sems.at[0]),
        pltpu.make_async_copy(mix_hbm, mix_ref, sems.at[1]),
    ]
    for e in range(3):
        copies.append(pltpu.make_async_copy(
            w_hbm.at[:, e], wide.at[:, :, pl.ds(e * channels, channels)], sems.at[2 + e]
        ))
    for copy in copies:
        copy.start()
    fill_rows(near_patch, 1, near_ref.at[0], columns, False)
    fill_rows(near_patch, side, far_ref.at[0], columns, False)
    fill_rows(far_patch, 1, far_ref.at[0], columns, False)
    fill_rows(far_patch, 2 - side, near_ref.at[0], columns, False)
    for copy in copies[:2]:
        copy.wait()
    near_pulled[...] = lax.dot_general(fg_ref[1 - parity], mix_ref[...], NT, preferred_element_type=f32)
    far_pulled[...] = lax.dot_general(fg_ref[parity], mix_ref[...], NT, preferred_element_type=f32)
    for copy in copies[2:]:
        copy.wait()
    for part, patch, a in ((near_part, near_patch, side), (far_part, far_patch, 2 - side)):
        taps = [3, 4, 5] + [a * 3 + b for b in range(3)]
        part[...] = join_columns(taps_dot(patch, wide, taps), 1, columns, place_ref[...])


def finish_plane(columns, place, patch, a, wide, part_ref, pulled_ref, fg, before_ref, hidden_ref, hg_ref, rows_ref):
    taps = [a * 3 + b for b in range(3)]
    summed = part_ref[...] + join_columns(taps_dot(patch, wide, taps), 1, columns, place)
    activate(summed, pulled_ref[...], hidden_ref, hg_ref)
    kernel_grads(columns, place, patch, hidden_ref, hg_ref, fg, rows_ref, before_ref)


def near_kernel(columns, place_ref, near_ref, far_ref, pair_ref, wide, fg_ref, part_ref, pulled_ref,
                hidden_ref, hg_ref, rows_ref, patch):
    parity, side = turn()
    fill_rows(patch, 2 - side, pair_ref.at[0], columns, False)
    fill_rows(patch, 1, near_ref.at[0], columns, False)
    fill_rows(patch, side, far_ref.at[0], columns, False)
    finish_plane(columns, place_ref[...], patch, 2 - side, wide, part_ref, pulled_ref, fg_ref[1 - parity], None,
                 hidden_ref, hg_ref, rows_ref)


def far_kernel(columns, order, place_ref, near_ref, far_ref, cross_ref, wide, fg_ref, part_ref, pulled_ref, before_ref,
               near_hg,
               hidden_ref, hg_ref, grads_ref, patch, rows_ref):
    parity, side = turn()
    fill_rows(patch, side, cross_ref.at[0], columns, False)
    clear_outside(patch, side)
    fill_rows(patch, 1, far_ref.at[0], columns, False)
    fill_rows(patch, 2 - side, near_ref.at[0], columns, False)
    finish_plane(columns, place_ref[...], patch, side, wide, part_ref, pulled_ref, fg_ref[parity], before_ref,
                 hidden_ref, hg_ref, rows_ref)
    if order is None:
        grads_ref[...] = rows_ref[...].astype(bf16)
    else:
        piece = grads_ref.shape[1]
        spots = order()
        for k, spot in enumerate(spots):
            grads_ref[spot] = rows_ref[pl.ds(k * piece, piece), :].astype(bf16)
        for spot, first, rows in runs_of(near_hg.shape[1], piece):
            grads_ref[len(spots) + spot, pl.ds(0, rows), :] = near_hg[0, pl.ds(first, rows), :]


def runs_of(cells, piece):
    step = piece // 16 * 16
    return [(spot, first, min(step, cells - first)) for spot, first in enumerate(range(0, cells, step))]


def split_kernel(start, kept_ref, came_ref, own_ref, *out_refs):
    lot = own_ref.shape[0]
    for chip in range(len(out_refs) + 1):
        for i in range(lot):
            at = chip * lot + i
            value = kept_ref[start + at].astype(f32) + came_ref[at].astype(f32)
            if chip == 0:
                own_ref[i] = value
            else:
                out_refs[chip - 1][i] = value.astype(bf16)


def gather_kernel(keeps, after_ref, own_ref, *refs):
    lot = own_ref.shape[0]
    came, out = refs[: len(refs) - lot], refs[len(refs) - lot :]
    for i in range(lot):
        value = own_ref[i]
        for ref in came:
            value = value + ref[i].astype(f32)
        out[i][...] = value if keeps and i == 0 else value.astype(bf16)


def backward_kernel(columns, place_ref, near_ref, far_ref, pair_ref, cross_ref, wide, mix_ref, near_hidden, far_hidden,
                    features_ref, input_ref, near_patch, far_patch, pair_plane):
    cells, channels = near_ref.shape[1:]
    if pair_ref.shape[1] == cells:
        pair_plane[...] = pair_ref[0]
    else:
        spots = runs_of(cells, pair_ref.shape[1])
        start = pair_ref.shape[0] - len(spots)
        for spot, first, rows in spots:
            pair_plane[pl.ds(first, rows), :] = pair_ref[start + spot, pl.ds(0, rows), :]
    parity, side = turn()
    features_ref[1 - parity] = jnp.dot(near_hidden[0], mix_ref[...], preferred_element_type=f32).astype(bf16)
    features_ref[parity] = jnp.dot(far_hidden[0], mix_ref[...], preferred_element_type=f32).astype(bf16)
    fill_rows(near_patch, side, pair_plane, columns, True)
    fill_rows(near_patch, 1, near_ref.at[0], columns, True)
    fill_rows(near_patch, 2 - side, far_ref.at[0], columns, True)
    fill_rows(far_patch, side, near_ref.at[0], columns, True)
    fill_rows(far_patch, 1, far_ref.at[0], columns, True)
    fill_rows(far_patch, 2 - side, cross_ref.at[0], columns, True)
    clear_outside(far_patch, 2 - side)
    for patch, plane in ((near_patch, 1 - parity), (far_patch, parity)):
        parts = jnp.zeros((near_ref.shape[1], 3 * channels), f32)
        for first in range(0, 9, 2):
            taps = range(first, min(first + 2, 9))
            block = jnp.concatenate(
                [
                    jnp.concatenate([wide[t, :, e * channels : (e + 1) * channels] for e in range(3)], axis=0)
                    for t in taps
                ],
                axis=1,
            )
            parts = parts + lax.dot_general(
                jnp.concatenate([patch[t] for t in taps], axis=1), block, NT, preferred_element_type=f32
            )
        input_ref[plane] = join_columns(parts, -1, columns, place_ref[...]).astype(bf16)


def digits_of(count):
    digits = []
    while count > 1:
        for radix in (2, 3, 5, 7, count) if not digits else (4, 2, 3, 5, 7, count):
            if count % radix == 0:
                digits.append(radix)
                count //= radix
                break
    return digits


def stages_of(axis, digits):
    stages, stride = [], 1
    for radix in digits:
        stages.append((axis, stride, radix))
        stride *= radix
    return stages


def apart(digit, mine, radix):
    if radix & (radix - 1) == 0:
        return lax.bitwise_xor(mine, digit)
    return lax.rem(digit - mine + radix, radix)


def send(value, stage, k):
    axis, stride, radix = stage
    pairs = []
    for i in range(lax.axis_size(axis)):
        digit = i // stride % radix
        other = digit ^ k if radix & (radix - 1) == 0 else (digit + k) % radix
        pairs.append((i, i + (other - digit) * stride))
    return lax.ppermute(value, axis, pairs)


def swaps(start, count):
    found = []
    for i in range(start, count + start, 2):
        found += [(i, (i + 1) % count), ((i + 1) % count, i)]
    return found


def shards(universes, conv_weight, mix_weight, feature_grad):
    channels = conv_weight.shape[1]
    width = mix_weight.shape[1]
    planes, map_rows, columns = universes.shape[1:4]
    if planes != 2 or lax.axis_size("space") % 2:
        raise ValueError("slab shape")
    cells = map_rows * columns
    group_count, slab_count = lax.axis_size("dp"), lax.axis_size("space")
    devices = group_count * slab_count
    space_digits = digits_of(slab_count)
    dp_digits = [4] if group_count == 4 else digits_of(group_count)
    stages = stages_of("space", space_digits) + stages_of("dp", dp_digits)

    x = universes.reshape(planes, cells, channels)
    fg = feature_grad.reshape(planes, cells, width)
    weights = conv_weight.reshape(9, 3, channels, channels)
    pair_swaps, cross_swaps = swaps(0, slab_count), swaps(1, slab_count)

    parity = lax.rem(lax.axis_index("space"), 2)
    x_near = lax.dynamic_slice_in_dim(x, 1 - parity, 1, 0)
    x_far = lax.dynamic_slice_in_dim(x, parity, 1, 0)
    x_cross = lax.ppermute(x_far, "space", cross_swaps)
    x_pair = lax.ppermute(x_near, "space", pair_swaps)

    total_rows = 27 * channels + channels * width // channels
    share = (total_rows * channels + devices - 1) // devices
    lots = (
        share * devices == total_rows * channels
        and share % channels == 0
        and len(stages) == 3
        and stages[0][2] == 2
        and stages[1][2] == 4
        and stages[2][2] == 4
    )
    if lots:
        piece = share // channels
        chips, groups = stages[1][2], stages[2][2]
        lot = groups // 2
        grads_shape = (devices + len(runs_of(cells, piece)), piece, channels)

        def order():
            def relative(stage):
                axis, stride, radix = stage
                mine = lax.rem(lax.div(lax.axis_index(axis), stride), radix)
                return [apart(digit, mine, radix) for digit in range(radix)]

            cores = [core * (2 * chips * lot) for core in relative(stages[0])]
            here = lax.rem(lax.div(lax.axis_index("space"), 2), 4)
            turned_round = jnp.logical_or(here == 1, here == 2)
            chip_spots = []
            for chip in relative(stages[1]):
                side = jnp.logical_or(chip == 1, chip == 2)
                chip_spots.append(lax.select(jnp.logical_and(turned_round, side), 3 - chip, chip) * lot)
            mine = lax.axis_index("dp")
            late = lax.div(mine, lot)
            group_spots = []
            for group in relative(stages[2]):
                near = 1 - lax.div(group, lot)
                group_spots.append(near * (chips * lot) + lax.rem(group + (1 - near) * late, lot))
            spots = []
            for k in range(devices):
                group, place = divmod(k, slab_count)
                chip, core = divmod(place, 2)
                spots.append(cores[core] + chip_spots[chip] + group_spots[group])
            return spots
    else:
        grads_shape = (total_rows, channels)
        order = None

    def like(*shape, dtype=bf16):
        return jax.ShapeDtypeStruct(shape, dtype)

    def params(mebibytes):
        return pltpu.CompilerParams(vmem_limit_bytes=mebibytes * 1024 * 1024)

    def cost(blocks, read):
        return pl.CostEstimate(
            flops=2 * cells * channels * channels * blocks, bytes_accessed=read, transcendentals=0
        )

    plane = like(1, cells, channels)
    plane_sum = like(cells, channels, dtype=f32)
    patch = pltpu.VMEM((9, cells, channels), bf16)
    place = pl.pallas_call(
        functools.partial(columns_kernel, columns),
        out_shape=like(cells, channels, dtype=jnp.int32),
        out_specs=VMEM,
        compiler_params=params(4),
        cost_estimate=cost(300, 8_000_000),
        name="columns_of_cells",
    )()
    near_part, far_part, near_pulled, far_pulled, wide, mix_near, fg_near = pl.pallas_call(
        functools.partial(inner_kernel, columns),
        out_shape=(plane_sum,) * 4
        + (like(9, channels, 3 * channels), like(*mix_weight.shape), like(*fg.shape)),
        in_specs=[VMEM] + [HBM] * 3 + [VMEM] * 2,
        out_specs=(VMEM,) * 7,
        scratch_shapes=[patch, patch, pltpu.SemaphoreType.DMA((5,))],
        compiler_params=params(16),
        cost_estimate=cost(44, 2_000_000),
        name="inner_taps",
    )(place, weights, mix_weight, fg, x_near, x_far)
    near_hidden, near_hg, near_rows = pl.pallas_call(
        functools.partial(near_kernel, columns),
        out_shape=(plane, plane, like(total_rows, channels, dtype=f32)),
        in_specs=[VMEM] * 8,
        out_specs=(VMEM,) * 3,
        scratch_shapes=[patch],
        compiler_params=params(16),
        cost_estimate=cost(38, 3_000_000),
        name="near_plane",
    )(place, x_near, x_far, x_pair, wide, fg_near, near_part, near_pulled)
    far_hidden, far_hg, grads = pl.pallas_call(
        functools.partial(far_kernel, columns, order),
        out_shape=(plane, plane, like(*grads_shape)),
        in_specs=[VMEM] * 10,
        out_specs=(VMEM,) * 3,
        scratch_shapes=[patch, pltpu.VMEM((total_rows, channels), f32)],
        compiler_params=params(16),
        cost_estimate=cost(38, 3_000_000),
        name="far_plane",
    )(place, x_near, x_far, x_cross, wide, fg_near, far_part, far_pulled, near_rows, near_hg)

    hg_cross = lax.ppermute(far_hg, "space", cross_swaps)
    if lots:
        size = devices // 4
        first = send(grads[2 * size : 3 * size], stages[0], 1)
        second = send(grads[3 * size :], stages[0], 1)
        hg_pair = second
    else:
        hg_pair = lax.ppermute(near_hg, "space", pair_swaps)
    features, input_grad = pl.pallas_call(
        functools.partial(backward_kernel, columns),
        out_shape=(like(planes, cells, width), like(planes, cells, channels)),
        in_specs=[VMEM] * 9,
        out_specs=(VMEM, VMEM),
        scratch_shapes=[patch, patch, pltpu.VMEM((cells, channels), bf16)],
        compiler_params=params(16),
        cost_estimate=cost(58, 2_000_000),
        name="features_and_input_grad",
    )(place, near_hg, far_hg, hg_pair, hg_cross, wide, mix_near, near_hidden, far_hidden)

    if lots:
        arrived = []
        for start, came, near in ((0, first, False), (size, second, True)):
            own, *others = pl.pallas_call(
                functools.partial(split_kernel, start),
                out_shape=[like(lot, piece, channels, dtype=f32)] + [like(lot, piece, channels)] * (chips - 1),
                in_specs=[VMEM, VMEM],
                out_specs=[VMEM] * chips,
                compiler_params=params(8),
                name="sum_of_core_pair",
            )(grads, came)
            came = [
                lax.ppermute(
                    others[k], "space", [(2 * a + core, 2 * b + core) for a, b in CHIP_ROUNDS[k] for core in range(2)]
                )
                for k in (1, 2, 0)
            ]
            parts = pl.pallas_call(
                functools.partial(gather_kernel, near),
                out_shape=[like(piece, channels, dtype=f32 if near and i == 0 else bf16) for i in range(lot)],
                in_specs=[pl.BlockSpec(memory_space=pl.ANY)] + [VMEM] * chips,
                out_specs=[VMEM] * lot,
                compiler_params=params(8),
                name="sum_of_chips",
            )(hg_cross, own, *came)
            if near:
                arrived += [parts[0], send(parts[1], stages[2], 1).astype(f32)]
            else:
                arrived += [lax.ppermute(part, "dp", pairs).astype(f32) for part, pairs in zip(parts, FAR_ROUNDS)]
        total = sum(arrived[1:], arrived[0])
    else:
        flat = grads.reshape(-1)
        flat = jnp.pad(flat, (0, share * devices - flat.size))
        held = flat.reshape(dp_digits[::-1] + space_digits[::-1] + [share])
        places = {}
        for spot, stage in enumerate(stages_of("dp", dp_digits)[::-1] + stages_of("space", space_digits)[::-1]):
            places[stage] = spot
            mine = lax.rem(lax.axis_index(stage[0]) // stage[1], stage[2])
            held = jnp.take(held, apart(jnp.arange(stage[2]), mine, stage[2]), axis=spot)
        parts = jnp.transpose(held, [places[stage] for stage in stages] + [len(stages)])
        for stage in stages:
            total = parts[0].astype(f32)
            for term in [send(parts[k], stage, k) for k in range(1, stage[2])]:
                total = total + term.astype(f32)
            parts = total.astype(bf16)
    weight_grads = (total / devices).reshape(-1)
    return (features.reshape(feature_grad.shape), input_grad.reshape(universes.shape), weight_grads)


def solution(mesh):
    return jax.shard_map(
        shards,
        mesh=mesh,
        in_specs=(P("dp", "space", None, None, None), P(), P(), P("dp", "space", None, None, None)),
        out_specs=(
            P("dp", "space", None, None, None),
            P("dp", "space", None, None, None),
            P(("dp", "space")),
        ),
        check_vma=False,
    )
```
